128 devices in a mesh: lat: 8 (over z, y_hi), lon: 16 (over y_lo, x, core).
Axes of the slice: x: 4, y: 4 (y_hi: 2, y_lo: 2; y = y_hi * 2 + y_lo), z: 4, core: 2. Of those that a mesh axis runs over, the one named last changes fastest.
Arguments:
- queries: bfloat16 [64, 768, 1024], P('lat', 'lon'), may hold values from -8 to 8
- key_vectors: bfloat16 [64, 768, 1024], P('lat', 'lon'), may hold values from -8 to 8
- value_vectors: bfloat16 [64, 768, 1024], P('lat', 'lon'), may hold values from -6 to 6
- cotangent: bfloat16 [64, 768, 1024], P('lat', 'lon'), may hold values from -6 to 6
- quad_weight: float32 [64], replicated, may hold values from 0.05 to 1
- lon_reach: int32 [64], P('lat'), may hold values from 1 to 96, as said below
Outputs:
- attended: bfloat16 [64, 768, 1024], P('lat', 'lon')
- grad_queries: bfloat16 [64, 768, 1024], P('lat', 'lon')
- grad_keys: bfloat16 [64, 768, 1024], P('lat', 'lon')
- grad_values: bfloat16 [64, 768, 1024], P('lat', 'lon')
The draws below stay inside these ranges and needn't reach their ends.
Inputs may be any that keep to these rules, and one draw needn't show every extreme that they name: `lon_reach`: in latitude rows 0 and 63 it equals 96.
All inputs are finite; a program needn't handle non-finite values.
Results may differ from the reference program's by a relative error of at most 0.034.
Values may be sent and summed in bfloat16 or wider, within the bound.
No kernel may reach another device: no remote copies, remote signals or barrier semaphores. Data moves between devices by JAX's collectives and lax.ppermute only.
A program may use at most 384 MiB of HBM per device.

```python
import math
import jax
import jax.numpy as jnp
from jax import lax

HEADS = 16
HEAD_DIM = 64
D = 1024
LON_DEV = 48
HALO = 2
SPAN = 2
NLAT = 64
NLON = 768


def draw_queries(key, part):
    key = jax.random.fold_in(key, 11)
    drawn = jnp.clip(jax.random.normal(key, (NLAT, NLON, D), jnp.float32), -5.0, 5.0)
    return drawn.astype(jnp.bfloat16)


def draw_key_vectors(key, part):
    key = jax.random.fold_in(key, 12)
    drawn = jnp.clip(jax.random.normal(key, (NLAT, NLON, D), jnp.float32), -5.0, 5.0)
    return drawn.astype(jnp.bfloat16)


def draw_lon_reach(key, part):
    key = jax.random.fold_in(key, 5)
    widest = SPAN * LON_DEV
    base = jax.random.randint(jax.random.fold_in(key, 6), (), max(1, LON_DEV // 4), LON_DEV // 2 + 1)
    jitter = jax.random.randint(jax.random.fold_in(key, 7), (NLAT,), 0, LON_DEV // 2 + 1)
    lat_rows = jnp.arange(NLAT, dtype=jnp.int32)
    polar = jnp.abs(2 * lat_rows - (NLAT - 1))
    full = (NLAT - 1) * (NLAT - 1)
    cosine_sq = (full - polar * polar) * 1024 // full
    candidates = jnp.arange(1, widest + 1, dtype=jnp.int32)
    short = jnp.sum(candidates[None, :] * candidates[None, :] * cosine_sq[:, None] < base * base * 1024, axis=1).astype(jnp.int32)
    reach = jnp.clip(short + jitter, 1, widest)
    at_pole = (lat_rows == 0) | (lat_rows == NLAT - 1)
    return jnp.where(at_pole, widest, reach).astype(jnp.int32)


def level_of(stream_key, shape, shards, smallest, high):
    def one(position, blocks):
        steps = jax.random.uniform(jax.random.fold_in(jax.random.fold_in(stream_key, 6), position), (blocks,), jnp.float32, smallest / len(shards), high / len(shards))
        return jnp.repeat(jnp.exp(steps), shape[position] // blocks).reshape((-1,) + (1,) * (len(shape) - position - 1))

    level = one(*shards[0])
    for cut in shards[1:]:
        level = level * one(*cut)
    return level


def noise(own_key, extent, spread, limit, pieces=(), kind=jnp.bfloat16):
    values = jax.random.normal(own_key, extent, jnp.float32) * spread
    if len(pieces) > 0:
        values = level_of(own_key, extent, pieces, -0.22, 0.18) * values
    return jnp.clip(values, min=-limit, max=limit).astype(kind)


def setup_inputs(seed: int = 0) -> dict:
    arg_keys = jax.random.split(jax.random.key(seed), 7)
    return {
        "queries": draw_queries(jax.random.fold_in(arg_keys[6], 71), 0),
        "key_vectors": draw_key_vectors(jax.random.fold_in(arg_keys[6], 71), 0),
        "value_vectors": noise(arg_keys[2], (NLAT, NLON, D), 1.0, 6.0, ((0, 8), (1, 16))),
        "cotangent": noise(arg_keys[3], (NLAT, NLON, D), 1.0, 6.0, ((0, 8), (1, 16))),
        "quad_weight": jnp.clip(jnp.exp(jax.random.uniform(arg_keys[4], (NLAT,), jnp.float32, math.log(0.05), math.log(1.0))), 0.05, 1.0),
        "lon_reach": draw_lon_reach(jax.random.fold_in(arg_keys[6], 71), 0),
    }


def window_allowed(query_rows, query_cols, key_rows, key_cols, lon_reach):
    lat_total = lon_reach.shape[0]
    rows_near = jnp.abs(query_rows[:, None] - key_rows[None, :]) <= HALO
    key_inside = (key_rows >= 0) & (key_rows < lat_total)
    query_inside = (query_rows >= 0) & (query_rows < lat_total)
    col_gap = jnp.abs(query_cols[:, None] - key_cols[None, :])
    col_gap = jnp.minimum(col_gap, NLON - col_gap)
    reach_cells = lon_reach[jnp.clip(query_rows, 0, lat_total - 1)]
    return rows_near & key_inside[None, :] & query_inside[:, None] & (col_gap <= reach_cells[:, None])


def rounded(source):
    return lax.optimization_barrier(source.astype(jnp.bfloat16)).astype(jnp.float32)


def split_heads(source):
    return source.reshape(-1, HEADS, HEAD_DIM).astype(jnp.float32)


def slice_rows(source, start, count):
    zero_index = jnp.zeros((), jnp.int32)
    starts = (jnp.asarray(start).astype(jnp.int32),) + (zero_index,) * (source.ndim - 1)
    return lax.dynamic_slice(source, starts, (count,) + source.shape[1:])


def reference(queries, key_vectors, value_vectors, cotangent, quad_weight, lon_reach):
    feature_width = queries.shape[-1]
    score_scale = float(HEAD_DIM) ** -0.5
    per_row = NLON // LON_DEV
    span_cols = SPAN * LON_DEV
    window_cols = LON_DEV + 2 * span_cols
    window_rows = 2 * HALO + 1
    row_pad = ((HALO, HALO), (0, 0), (0, 0))
    padded_keys = jnp.pad(key_vectors, row_pad)
    padded_values = jnp.pad(value_vectors, row_pad)
    padded_queries = jnp.pad(queries, row_pad)
    padded_cot = jnp.pad(cotangent, row_pad)
    padded_weight = jnp.pad(quad_weight, HALO)
    window_offsets = jnp.arange(window_cols, dtype=jnp.int32) - span_cols
    slab_rows = jnp.arange(window_rows, dtype=jnp.int32) - HALO

    def window(source, lat_row, first_col):
        row_slab = slice_rows(source, lat_row, window_rows)
        col_ids = ((first_col + window_offsets) % NLON).astype(jnp.int32)
        return jnp.take(row_slab, col_ids, axis=1), col_ids

    def own_block(source, lat_row, first_col):
        zero_index = jnp.zeros((), jnp.int32)
        return lax.dynamic_slice(source, (lat_row.astype(jnp.int32), first_col.astype(jnp.int32), zero_index),
                                 (1, LON_DEV, source.shape[-1]))

    def first_pass(flat_index):
        lat_row = (flat_index // per_row).astype(jnp.int32)
        first_col = ((flat_index % per_row) * LON_DEV).astype(jnp.int32)
        own_cols = first_col + jnp.arange(LON_DEV, dtype=jnp.int32)
        query_heads = split_heads(own_block(queries, lat_row, first_col))
        cot_heads = split_heads(own_block(cotangent, lat_row, first_col))
        key_slab, col_ids = window(padded_keys, lat_row, first_col)
        value_slab = window(padded_values, lat_row, first_col)[0]
        key_heads = split_heads(key_slab)
        value_heads = split_heads(value_slab)
        key_weight = jnp.repeat(slice_rows(padded_weight, lat_row, window_rows), window_cols)
        key_rows = jnp.repeat(lat_row + slab_rows, window_cols)
        key_cols = jnp.tile(col_ids, window_rows)
        query_rows = jnp.full((LON_DEV,), lat_row, jnp.int32)
        allowed = window_allowed(query_rows, own_cols, key_rows, key_cols, lon_reach)
        scores = jnp.einsum("qhd,khd->hqk", query_heads, key_heads) * score_scale
        maxima = jnp.max(jnp.where(allowed, scores, -jnp.inf), axis=-1)
        weights = key_weight * jnp.exp(jnp.where(allowed, scores - maxima[..., None], -jnp.inf))
        totals = jnp.sum(weights, axis=-1)
        summed = jnp.einsum("hqk,khd->qhd", rounded(weights), value_heads)
        attended = lax.optimization_barrier((summed / totals.T[..., None]).astype(jnp.bfloat16))
        deltas = jnp.sum(cot_heads * attended.astype(jnp.float32), axis=-1).T
        log_totals = maxima + jnp.log(totals)
        probs = key_weight * jnp.exp(jnp.where(allowed, scores - log_totals[..., None], -jnp.inf))
        prob_grads = jnp.einsum("qhd,khd->hqk", cot_heads, value_heads)
        score_grads = rounded(probs * (prob_grads - deltas[..., None]))
        grad_query = jnp.einsum("hqk,khd->qhd", score_grads, key_heads) * score_scale
        return (attended.reshape(LON_DEV, feature_width),
                grad_query.reshape(LON_DEV, feature_width).astype(jnp.bfloat16),
                log_totals.T, deltas.T)

    block_ids = jnp.arange(NLAT * per_row, dtype=jnp.int32)
    attended, grad_queries, log_rows, delta_rows = lax.map(first_pass, block_ids)

    def to_grid(source):
        return source.reshape(NLAT, NLON, source.shape[-1])

    padded_logs = jnp.pad(to_grid(log_rows), row_pad)
    padded_deltas = jnp.pad(to_grid(delta_rows), row_pad)

    def second_pass(flat_index):
        lat_row = (flat_index // per_row).astype(jnp.int32)
        first_col = ((flat_index % per_row) * LON_DEV).astype(jnp.int32)
        own_cols = first_col + jnp.arange(LON_DEV, dtype=jnp.int32)
        key_heads = split_heads(own_block(key_vectors, lat_row, first_col))
        value_heads = split_heads(own_block(value_vectors, lat_row, first_col))
        key_weight = slice_rows(quad_weight, lat_row, 1)
        query_slab, col_ids = window(padded_queries, lat_row, first_col)
        query_heads = split_heads(query_slab)
        cot_heads = split_heads(window(padded_cot, lat_row, first_col)[0])
        log_slab = window(padded_logs, lat_row, first_col)[0].reshape(-1, HEADS).T
        delta_slab = window(padded_deltas, lat_row, first_col)[0].reshape(-1, HEADS).T
        query_rows = jnp.repeat(lat_row + slab_rows, window_cols)
        query_cols = jnp.tile(col_ids, window_rows)
        key_rows = jnp.full((LON_DEV,), lat_row, jnp.int32)
        allowed = window_allowed(query_rows, query_cols, key_rows, own_cols, lon_reach)
        scores = jnp.einsum("qhd,khd->hqk", query_heads, key_heads) * score_scale
        probs = key_weight * jnp.exp(jnp.where(allowed, scores - log_slab[..., None], -jnp.inf))
        prob_grads = jnp.einsum("qhd,khd->hqk", cot_heads, value_heads)
        score_grads = rounded(probs * (prob_grads - delta_slab[..., None]))
        grad_key = jnp.einsum("hqk,qhd->khd", score_grads, query_heads) * score_scale
        grad_value = jnp.einsum("hqk,qhd->khd", rounded(probs), cot_heads)
        return (grad_key.reshape(LON_DEV, feature_width).astype(jnp.bfloat16),
                grad_value.reshape(LON_DEV, feature_width).astype(jnp.bfloat16))

    grad_keys, grad_values = lax.map(second_pass, block_ids)
    return to_grid(attended), to_grid(grad_queries), to_grid(grad_keys), to_grid(grad_values)
```

```python
import jax
import jax.numpy as jnp
from jax import lax
from jax.experimental import pallas as pl
from jax.experimental.pallas import tpu as pltpu
from jax.sharding import PartitionSpec as P

HEADS = 16
HEAD_DIM = 64
HALO = 2
REACH = 96
QBLOCK = 128
FAR = -1e30
VMEM_BYTES = 56 * 1024 * 1024
NT = (((1,), (1,)), ((), ()))


def vmem():
    return pl.BlockSpec(memory_space=pltpu.VMEM)


def smem():
    return pl.BlockSpec(memory_space=pltpu.SMEM)


def pack_pair(left, right):
    rows, cols, width = left.shape
    heads = width // HEAD_DIM

    def body(left_ref, right_ref, out_ref):
        for h in range(heads):
            at = slice(h * HEAD_DIM, (h + 1) * HEAD_DIM)
            out_ref[h, 0] = jnp.concatenate([left_ref[0, :, at], right_ref[0, :, at]], axis=-1)

    block = pl.BlockSpec((1, cols, width), lambda r: (r, 0, 0))
    return pl.pallas_call(
        body,
        grid=(rows,),
        in_specs=[block, block],
        out_specs=pl.BlockSpec((heads, 1, cols, 2 * HEAD_DIM), lambda r: (0, r, 0, 0)),
        out_shape=jax.ShapeDtypeStruct((heads, rows, cols, 2 * HEAD_DIM), left.dtype),
    )(left, right)


def unpack_pair(packed):
    heads, rows, cols, _ = packed.shape
    width = heads * HEAD_DIM

    def body(in_ref, left_ref, right_ref):
        for h in range(heads):
            at = slice(h * HEAD_DIM, (h + 1) * HEAD_DIM)
            left_ref[0, :, at] = in_ref[h, 0, :, :HEAD_DIM]
            right_ref[0, :, at] = in_ref[h, 0, :, HEAD_DIM:]

    block = pl.BlockSpec((1, cols, width), lambda r: (r, 0, 0))
    shape = jax.ShapeDtypeStruct((rows, cols, width), packed.dtype)
    return pl.pallas_call(
        body,
        grid=(rows,),
        in_specs=[pl.BlockSpec((heads, 1, cols, 2 * HEAD_DIM), lambda r: (0, r, 0, 0))],
        out_specs=[block, block],
        out_shape=[shape, shape],
    )(packed)


def attend(reach, log_weight, kv, kv_above, kv_below, qc):
    sectors, rows, cols, lanes = kv.shape
    ring = sectors * cols
    ext_rows = rows + 2 * HALO
    taps = 2 * HALO + 1
    padded = ring + 2 * REACH
    window = QBLOCK + 2 * REACH
    blocks = ring // QBLOCK
    scale = float(HEAD_DIM) ** -0.5

    def body(reach_ref, logw_ref, kv_ref, above_ref, below_ref, qc_ref,
             qo_ref, mid_ref, edge_ref, up_ref, down_ref,
             kvw, kvt, qcw, dkv, sd, bias, qow):
        for s in range(sectors):
            at = slice(REACH + s * cols, REACH + (s + 1) * cols)
            kvw[0:HALO, at] = above_ref[s]
            kvw[HALO:HALO + rows, at] = kv_ref[s]
            kvw[HALO + rows:ext_rows, at] = below_ref[s]
            qcw[:, s * cols:(s + 1) * cols] = qc_ref[s]
        kvw[:, 0:REACH] = kvw[:, ring:ring + REACH]
        kvw[:, REACH + ring:padded] = kvw[:, REACH:2 * REACH]

        @pl.loop(0, ext_rows)
        def _(kr):
            kvt[kr] = kvw[kr].T
            dkv[kr] = jnp.zeros((padded, lanes), jnp.float32)

        lane = lax.broadcasted_iota(jnp.int32, (QBLOCK, lanes), 1)

        @pl.loop(0, rows)
        def _(r):
            gap = (lax.broadcasted_iota(jnp.int32, (window, QBLOCK), 0) - REACH
                   - lax.broadcasted_iota(jnp.int32, (window, QBLOCK), 1))
            near = jnp.abs(gap) <= reach_ref[r]
            for w in range(taps):
                bias[w] = jnp.where(near, logw_ref[r + w], FAR)

            @pl.loop(0, blocks)
            def _(b):
                start = pl.multiple_of(b * QBLOCK, QBLOCK)
                span = pl.ds(start, window)
                rows_qc = qcw[r, pl.ds(start, QBLOCK), :]
                zero = jnp.zeros_like(rows_qc)
                qb = jnp.concatenate(
                    [jnp.where(lane < HEAD_DIM, rows_qc * scale, zero),
                     jnp.where(lane < HEAD_DIM, zero, rows_qc)], axis=0)
                top = jnp.full((8, QBLOCK), FAR, jnp.float32)
                for w in range(taps):
                    both = lax.dot_general(kvw[r + w, span, :], qb, NT,
                                           preferred_element_type=jnp.float32)
                    score = both[:, :QBLOCK] + bias[w]
                    sd[w, :, :QBLOCK] = score
                    sd[w, :, QBLOCK:] = both[:, QBLOCK:]
                    top = jnp.maximum(top, jnp.max(score.reshape(window // 8, 8, QBLOCK), axis=0))
                top = jnp.max(top, axis=0, keepdims=True)
                total = jnp.zeros((8, QBLOCK), jnp.float32)
                dot = jnp.zeros((8, QBLOCK), jnp.float32)
                for w in range(taps):
                    p = jnp.exp(sd[w, :, :QBLOCK] - top)
                    sd[w, :, :QBLOCK] = p
                    total += jnp.sum(p.reshape(window // 8, 8, QBLOCK), axis=0)
                    dot += jnp.sum((p * sd[w, :, QBLOCK:]).reshape(window // 8, 8, QBLOCK), axis=0)
                inverse = 1.0 / jnp.sum(total, axis=0, keepdims=True)
                delta = jnp.sum(dot, axis=0, keepdims=True) * inverse
                dq = jnp.zeros((HEAD_DIM, QBLOCK), jnp.float32)
                out = jnp.zeros((HEAD_DIM, QBLOCK), jnp.float32)
                for w in range(taps):
                    prob = sd[w, :, :QBLOCK] * inverse
                    ds = (prob * (sd[w, :, QBLOCK:] - delta)).astype(jnp.bfloat16)
                    pb = prob.astype(jnp.bfloat16)
                    dq += jnp.dot(kvt[r + w, :HEAD_DIM, span], ds, preferred_element_type=jnp.float32)
                    out += jnp.dot(kvt[r + w, HEAD_DIM:, span], pb, preferred_element_type=jnp.float32)
                    dkv[r + w, span, :] += jnp.dot(jnp.concatenate([ds, pb], axis=1), qb,
                                                   preferred_element_type=jnp.float32)
                qo = jnp.concatenate([dq * scale, out], axis=0)
                qow[r, pl.ds(start, QBLOCK), :] = qo.T.astype(jnp.bfloat16)

        dkv[:, ring:ring + REACH] += dkv[:, 0:REACH]
        dkv[:, REACH:2 * REACH] += dkv[:, REACH + ring:padded]
        for s in range(sectors):
            at = slice(REACH + s * cols, REACH + (s + 1) * cols)
            qo_ref[s] = qow[:, s * cols:(s + 1) * cols]
            up_ref[s] = dkv[0:HALO, at].astype(jnp.bfloat16)
            edge_ref[s, :HALO] = dkv[HALO:2 * HALO, at].astype(jnp.bfloat16)
            mid_ref[s] = dkv[2 * HALO:rows, at].astype(jnp.bfloat16)
            edge_ref[s, HALO:] = dkv[rows:rows + HALO, at].astype(jnp.bfloat16)
            down_ref[s] = dkv[rows + HALO:ext_rows, at].astype(jnp.bfloat16)

    def out(count):
        return jax.ShapeDtypeStruct((sectors, count, cols, lanes), jnp.bfloat16)

    return pl.pallas_call(
        body,
        in_specs=[smem(), smem(), vmem(), vmem(), vmem(), vmem()],
        out_specs=[vmem()] * 5,
        out_shape=[out(rows), out(rows - 2 * HALO), out(2 * HALO), out(HALO), out(HALO)],
        scratch_shapes=[
            pltpu.VMEM((ext_rows, padded, lanes), jnp.bfloat16),
            pltpu.VMEM((ext_rows, lanes, padded), jnp.bfloat16),
            pltpu.VMEM((rows, ring, lanes), jnp.bfloat16),
            pltpu.VMEM((ext_rows, padded, lanes), jnp.float32),
            pltpu.VMEM((taps, window, 2 * QBLOCK), jnp.float32),
            pltpu.VMEM((taps, window, QBLOCK), jnp.float32),
            pltpu.VMEM((rows, ring, lanes), jnp.bfloat16),
        ],
        compiler_params=pltpu.CompilerParams(vmem_limit_bytes=VMEM_BYTES),
    )(reach, log_weight, kv, kv_above, kv_below, qc)


def exchange(packed):
    return lax.all_to_all(packed, "lon", 0, 0)


def to_next_band(block, step):
    bands = lax.axis_size("lat")
    return lax.ppermute(block, "lat", [(i, i + step) for i in range(bands) if 0 <= i + step < bands])


def on_device(queries, key_vectors, value_vectors, cotangent, quad_weight, lon_reach):
    rows = queries.shape[0]
    ext = lax.axis_index("lat") * rows + jnp.arange(rows + 2 * HALO, dtype=jnp.int32) - HALO
    inside = (ext >= 0) & (ext < quad_weight.shape[0])
    log_weight = jnp.where(inside, jnp.log(quad_weight[jnp.clip(ext, 0, quad_weight.shape[0] - 1)]), FAR)

    kv = exchange(pack_pair(key_vectors, value_vectors))
    qc = exchange(pack_pair(queries, cotangent))
    above = to_next_band(kv[:, rows - HALO:], 1)
    below = to_next_band(kv[:, :HALO], -1)
    qo, mid, edge, up, down = attend(lon_reach, log_weight, kv, above, below, qc)
    from_below = to_next_band(up, -1)
    from_above = to_next_band(down, 1)
    grad_queries, attended = unpack_pair(exchange(qo))
    mid = exchange(mid)
    home = jnp.concatenate([from_above, from_below], axis=1).astype(jnp.float32)
    edge = exchange((edge.astype(jnp.float32) + home).astype(jnp.bfloat16))
    whole = jnp.concatenate([edge[:, :HALO], mid, edge[:, HALO:]], axis=1)
    grad_keys, grad_values = unpack_pair(whole)
    return attended, grad_queries, grad_keys, grad_values


def solution(mesh):
    cells = P("lat", "lon", None)
    return jax.shard_map(
        on_device,
        mesh=mesh,
        in_specs=(cells, cells, cells, cells, P(), P("lat")),
        out_specs=(cells, cells, cells, cells),
        check_vma=False,
    )
```

```python
import jax
import jax.numpy as jnp
from jax import lax
from jax.experimental import pallas as pl
from jax.experimental.pallas import tpu as pltpu
from jax.sharding import PartitionSpec as P

HEADS = 16
HEAD_DIM = 64
HALO = 2
REACH = 96
HALF = 64
TAPS = 2 * HALO + 2
WINDOW = HALF + 2 * REACH
INTERLEAVE = 4
FAR = -1e30
VMEM_BYTES = 56 * 1024 * 1024
NT = (((1,), (1,)), ((), ()))


def vmem():
    return pl.BlockSpec(memory_space=pltpu.VMEM)


def smem():
    return pl.BlockSpec(memory_space=pltpu.SMEM)


def pack_pair(left, right, row_block, step):
    _, cols, width = left.shape
    heads = width // HEAD_DIM

    def body(left_ref, right_ref, out_ref):
        for i in range(step):
            for h in range(heads):
                at = slice(h * HEAD_DIM, (h + 1) * HEAD_DIM)
                out_ref[h, i] = jnp.concatenate([left_ref[i, :, at], right_ref[i, :, at]], axis=-1)

    count = len(row_block)

    def source(i):
        row = jnp.int32(row_block[0])
        for n in range(1, count):
            row = jnp.where(i == n, row_block[n], row)
        return (row, 0, 0)

    block = pl.BlockSpec((step, cols, width), source)
    return pl.pallas_call(
        body,
        grid=(count,),
        in_specs=[block, block],
        out_specs=pl.BlockSpec((heads, step, cols, 2 * HEAD_DIM), lambda i: (0, i, 0, 0)),
        out_shape=jax.ShapeDtypeStruct((heads, count * step, cols, 2 * HEAD_DIM), left.dtype),
    )(left, right)


def split_heads(in_ref, left_ref, right_ref):
    heads, step = in_ref.shape[:2]
    for i in range(step):
        for pair in range(heads // 2):
            first, second = in_ref[2 * pair, i], in_ref[2 * pair + 1, i]
            at = slice(pair * 2 * HEAD_DIM, (pair + 1) * 2 * HEAD_DIM)
            left_ref[i, :, at] = jnp.concatenate([first[:, :HEAD_DIM], second[:, :HEAD_DIM]], axis=1)
            right_ref[i, :, at] = jnp.concatenate([first[:, HEAD_DIM:], second[:, HEAD_DIM:]], axis=1)


def unpack_edge(packed, rows):
    heads, _, cols, lanes = packed.shape
    width = heads * HEAD_DIM
    out = pl.BlockSpec((HALO, cols, width), lambda i: (i * (rows // HALO - 1), 0, 0))
    shape = jax.ShapeDtypeStruct((rows, cols, width), packed.dtype)
    return pl.pallas_call(
        split_heads,
        grid=(2,),
        in_specs=[pl.BlockSpec((heads, HALO, cols, lanes), lambda i: (0, i, 0, 0))],
        out_specs=[out, out],
        out_shape=[shape, shape],
    )(packed)


def unpack_rest(packed, grad_queries, attended):
    heads, _, cols, lanes = packed.shape
    rows, _, width = attended.shape
    half = (rows - 2 * HALO) // HALO

    def body(in_ref, _, __, dq_ref, out_ref, dk_ref, dv_ref):
        step = pl.program_id(0)

        @pl.when(step < half)
        def _():
            split_heads(in_ref, dq_ref, out_ref)

        @pl.when(step >= half)
        def _():
            split_heads(in_ref, dk_ref, dv_ref)

    def query_row(i):
        return (jnp.minimum(i, half - 1) + 1, 0, 0)

    def key_row(i):
        mid = jnp.maximum(i, half) - half + 1
        return (jnp.where(i < 2 * half, mid, jnp.where(i == 2 * half, 0, half + 1)), 0, 0)

    shape = jax.ShapeDtypeStruct((rows, cols, width), packed.dtype)
    query_block = pl.BlockSpec((HALO, cols, width), query_row)
    key_block = pl.BlockSpec((HALO, cols, width), key_row)
    held = pl.BlockSpec(memory_space=pl.ANY)
    return pl.pallas_call(
        body,
        grid=(2 * half + 2,),
        in_specs=[pl.BlockSpec((heads, HALO, cols, lanes), lambda i: (0, i, 0, 0)), held, held],
        out_specs=[query_block, query_block, key_block, key_block],
        out_shape=[shape] * 4,
        input_output_aliases={1: 0, 2: 1},
    )(packed, grad_queries, attended)


def two_pairs(reach_ref, logw_ref, kvw, kvt, qcw, dkv, sd, bias, qow, key_stride, own_first, own_stride, ext_first):
    lanes = kvw.shape[-1]
    blocks = qcw.shape[1] // HALF
    both = 2 * HALF
    scale = float(HEAD_DIM) ** -0.5
    lane = lax.broadcasted_iota(jnp.int32, (both, lanes), 1)

    @pl.loop(0, 2)
    def _(pair):
        base = pair * key_stride
        own = own_first + pair * own_stride
        r = 2 * pair
        key = lax.broadcasted_iota(jnp.int32, (WINDOW, both), 0) - REACH
        query = lax.broadcasted_iota(jnp.int32, (WINDOW, both), 1)
        second = query >= HALF
        gap = jnp.abs(key - jnp.where(second, query - HALF, query))
        near = gap <= jnp.where(second, reach_ref[own + 1], reach_ref[own])
        for w in range(TAPS):
            ok = near
            if w == 0:
                ok = near & jnp.logical_not(second)
            if w == TAPS - 1:
                ok = near & second
            bias[w] = jnp.where(ok, logw_ref[ext_first + base + w], FAR)

        @pl.loop(0, blocks // INTERLEAVE)
        def _(group):
            held = []
            for j in range(INTERLEAVE):
                block = group * INTERLEAVE + j
                start = pl.multiple_of(block * HALF, HALF)
                span = pl.ds(start, WINDOW)
                turned = pl.ds(pl.multiple_of(start - (j % 2) * HALF, both), WINDOW)
                rows_qc = jnp.concatenate(
                    [qcw[r, pl.ds(start, HALF), :], qcw[r + 1, pl.ds(start, HALF), :]], axis=0)
                zero = jnp.zeros_like(rows_qc)
                qb = jnp.concatenate(
                    [jnp.where(lane < HEAD_DIM, rows_qc * scale, zero),
                     jnp.where(lane < HEAD_DIM, zero, rows_qc)], axis=0)
                held.append((start, span, turned, qb))
            tops = []
            for j in range(INTERLEAVE):
                _, span, _, qb = held[j]
                top = jnp.full((8, both), FAR, jnp.float32)
                for w in range(TAPS):
                    product = lax.dot_general(kvw[base + w, span, :], qb, NT,
                                              preferred_element_type=jnp.float32)
                    score = product[:, :both] + bias[w]
                    sd[j, w, :, :both] = score
                    sd[j, w, :, both:] = product[:, both:]
                    top = jnp.maximum(top, jnp.max(score.reshape(WINDOW // 8, 8, both), axis=0))
                tops.append(jnp.max(top, axis=0, keepdims=True))
            sums = []
            for j in range(INTERLEAVE):
                total = jnp.zeros((8, both), jnp.float32)
                dot = jnp.zeros((8, both), jnp.float32)
                for w in range(TAPS):
                    p = jnp.exp(sd[j, w, :, :both] - tops[j])
                    sd[j, w, :, :both] = p
                    total += jnp.sum(p.reshape(WINDOW // 8, 8, both), axis=0)
                    dot += jnp.sum((p * sd[j, w, :, both:]).reshape(WINDOW // 8, 8, both), axis=0)
                inverse = 1.0 / jnp.sum(total, axis=0, keepdims=True)
                sums.append((inverse, jnp.sum(dot, axis=0, keepdims=True) * inverse))
            for j in range(INTERLEAVE):
                start, span, turned, qb = held[j]
                inverse, delta = sums[j]
                acc = jnp.zeros((lanes, 2 * both), jnp.float32)
                for w in range(TAPS):
                    prob = sd[j, w, :, :both] * inverse
                    ds = (prob * (sd[j, w, :, both:] - delta)).astype(jnp.bfloat16)
                    dp = jnp.concatenate([ds, prob.astype(jnp.bfloat16)], axis=1)
                    acc += jnp.dot(kvt[j % 2, base + w, :, turned], dp, preferred_element_type=jnp.float32)
                    dkv[base + w, span, :] += jnp.dot(dp, qb, preferred_element_type=jnp.float32)
                qo = jnp.concatenate([acc[:HEAD_DIM, :both] * scale, acc[HEAD_DIM:, both:]], axis=0)
                qo = qo.T.astype(jnp.bfloat16)
                qow[r, pl.ds(start, HALF), :] = qo[:HALF]
                qow[r + 1, pl.ds(start, HALF), :] = qo[HALF:]


def wrap_and_turn(kvw, kvt):
    key_rows, padded, _ = kvw.shape
    ring = padded - 2 * REACH
    kvw[:, 0:REACH] = kvw[:, ring:ring + REACH]
    kvw[:, REACH + ring:padded] = kvw[:, REACH:2 * REACH]

    @pl.loop(0, key_rows)
    def _(kr):
        kvt[0, kr] = kvw[kr].T
        kvt[1, kr, :, 0:padded - HALF] = kvw[kr, HALF:].T


def fold(dkv):
    padded = dkv.shape[1]
    ring = padded - 2 * REACH
    dkv[:, ring:ring + REACH] += dkv[:, 0:REACH]
    dkv[:, REACH:2 * REACH] += dkv[:, REACH + ring:padded]


def scratch(key_rows, ring, lanes):
    padded = ring + 2 * REACH
    return [
        pltpu.VMEM((key_rows, padded, lanes), jnp.bfloat16),
        pltpu.VMEM((2, key_rows, lanes, padded), jnp.bfloat16),
        pltpu.VMEM((4, ring, lanes), jnp.bfloat16),
        pltpu.VMEM((key_rows, padded, lanes), jnp.float32),
        pltpu.VMEM((INTERLEAVE, TAPS, WINDOW, 4 * HALF), jnp.float32),
        pltpu.VMEM((TAPS, WINDOW, 2 * HALF), jnp.float32),
        pltpu.VMEM((4, ring, lanes), jnp.bfloat16),
    ]


def params():
    return pltpu.CompilerParams(vmem_limit_bytes=VMEM_BYTES)


def cost():
    return pl.CostEstimate(flops=20_000_000_000, bytes_accessed=8_000_000, transcendentals=5_000_000)


def attend_edge(reach, log_weight, kv, kv_above, kv_below, qc):
    sectors, rows, cols, lanes = kv.shape
    ring = sectors * cols
    ext_rows = rows + 2 * HALO

    def body(reach_ref, logw_ref, kv_ref, above_ref, below_ref, qc_ref, qo_ref, up_ref, down_ref, part_ref,
             kvw, kvt, qcw, dkv, sd, bias, qow):
        for s in range(sectors):
            at = slice(REACH + s * cols, REACH + (s + 1) * cols)
            kvw[0:HALO, at] = above_ref[s]
            kvw[HALO:HALO + rows, at] = kv_ref[s]
            kvw[HALO + rows:ext_rows, at] = below_ref[s]
            qcw[:, s * cols:(s + 1) * cols] = qc_ref[s]
        wrap_and_turn(kvw, kvt)

        @pl.loop(0, ext_rows)
        def _(kr):
            dkv[kr] = jnp.zeros(dkv.shape[1:], jnp.float32)

        two_pairs(reach_ref, logw_ref, kvw, kvt, qcw, dkv, sd, bias, qow,
                  rows - HALO, 0, rows - HALO, 0)
        fold(dkv)
        part_ref[...] = dkv[HALO:HALO + rows, REACH:REACH + ring]
        for s in range(sectors):
            at = slice(REACH + s * cols, REACH + (s + 1) * cols)
            qo_ref[s] = qow[:, s * cols:(s + 1) * cols]
            up_ref[s] = dkv[0:HALO, at].astype(jnp.bfloat16)
            down_ref[s] = dkv[rows + HALO:ext_rows, at].astype(jnp.bfloat16)

    def out(count):
        return jax.ShapeDtypeStruct((sectors, count, cols, lanes), jnp.bfloat16)

    return pl.pallas_call(
        body,
        in_specs=[smem(), smem(), vmem(), vmem(), vmem(), vmem()],
        out_specs=[vmem()] * 4,
        out_shape=[out(4), out(HALO), out(HALO), jax.ShapeDtypeStruct((rows, ring, lanes), jnp.float32)],
        scratch_shapes=scratch(ext_rows, ring, lanes),
        compiler_params=params(),
        cost_estimate=cost(),
    )(reach, log_weight, kv, kv_above, kv_below, qc)


def attend_mid(reach, log_weight, kv, qc, part):
    sectors, rows, cols, lanes = kv.shape
    ring = sectors * cols
    padded = ring + 2 * REACH

    def body(reach_ref, logw_ref, kv_ref, qc_ref, part_ref, out_ref, kvw, kvt, qcw, dkv, sd, bias, qow):
        for s in range(sectors):
            at = slice(REACH + s * cols, REACH + (s + 1) * cols)
            kvw[:, at] = kv_ref[s]
            qcw[:, s * cols:(s + 1) * cols] = qc_ref[s]
        wrap_and_turn(kvw, kvt)

        @pl.loop(0, rows)
        def _(kr):
            dkv[kr, 0:REACH] = jnp.zeros((REACH, lanes), jnp.float32)
            dkv[kr, REACH:REACH + ring] = part_ref[kr]
            dkv[kr, REACH + ring:padded] = jnp.zeros((REACH, lanes), jnp.float32)

        two_pairs(reach_ref, logw_ref, kvw, kvt, qcw, dkv, sd, bias, qow, HALO, HALO, HALO, HALO)
        fold(dkv)
        for s in range(sectors):
            at = slice(REACH + s * cols, REACH + (s + 1) * cols)
            out_ref[s, 0:4] = qow[:, s * cols:(s + 1) * cols]
            out_ref[s, 4:8] = dkv[HALO:rows - HALO, at].astype(jnp.bfloat16)
            out_ref[s, 8:10] = dkv[0:HALO, at].astype(jnp.bfloat16)
            out_ref[s, 10:12] = dkv[rows - HALO:rows, at].astype(jnp.bfloat16)

    return pl.pallas_call(
        body,
        in_specs=[smem(), smem(), vmem(), vmem(), vmem()],
        out_specs=vmem(),
        out_shape=jax.ShapeDtypeStruct((sectors, 12, cols, lanes), jnp.bfloat16),
        scratch_shapes=scratch(rows, ring, lanes),
        compiler_params=params(),
        cost_estimate=cost(),
    )(reach, log_weight, kv, qc, part)


def exchange(packed):
    return lax.all_to_all(packed, "lon", 0, 0)


def to_next_band(block, step):
    bands = lax.axis_size("lat")
    return lax.ppermute(block, "lat", [(i, i + step) for i in range(bands) if 0 <= i + step < bands])


def on_device(queries, key_vectors, value_vectors, cotangent, quad_weight, lon_reach):
    rows = queries.shape[0]
    ext = lax.axis_index("lat") * rows + jnp.arange(rows + 2 * HALO, dtype=jnp.int32) - HALO
    inside = (ext >= 0) & (ext < quad_weight.shape[0])
    log_weight = jnp.where(inside, jnp.log(quad_weight[jnp.clip(ext, 0, quad_weight.shape[0] - 1)]), FAR)

    kv = exchange(pack_pair(key_vectors, value_vectors, (0, 1), rows // 2))
    qc_edge = exchange(pack_pair(queries, cotangent, (0, rows // HALO - 1), HALO))
    above = to_next_band(kv[:, rows - HALO:], 1)
    below = to_next_band(kv[:, :HALO], -1)
    qc_mid = exchange(pack_pair(queries, cotangent, (1, 2), HALO))
    qo_edge, up, down, part = attend_edge(lon_reach, log_weight, kv, above, below, qc_edge)
    from_below = to_next_band(up, -1)
    from_above = to_next_band(down, 1)
    grad_queries, attended = unpack_edge(exchange(qo_edge), rows)
    rest = attend_mid(lon_reach, log_weight, kv, qc_mid, part)
    home = jnp.concatenate([from_above, from_below], axis=1).astype(jnp.float32)
    edge = (rest[:, 8:].astype(jnp.float32) + home).astype(jnp.bfloat16)
    rest = exchange(lax.dynamic_update_slice(rest, edge, (0, 8, 0, 0)))
    grad_queries, attended, grad_keys, grad_values = unpack_rest(rest, grad_queries, attended)
    return attended, grad_queries, grad_keys, grad_values


def solution(mesh):
    cells = P("lat", "lon", None)
    return jax.shard_map(
        on_device,
        mesh=mesh,
        in_specs=(cells, cells, cells, cells, P(), P("lat")),
        out_specs=(cells, cells, cells, cells),
        check_vma=False,
    )
```

```python
import jax
import jax.numpy as jnp
from jax import lax
from jax.experimental import pallas as pl
from jax.experimental.pallas import tpu as pltpu
from jax.sharding import PartitionSpec as P

HEADS = 16
HEAD_DIM = 64
HALO = 2
REACH = 96
HALF = 64
TAPS = 2 * HALO + 2
WINDOW = HALF + 2 * REACH
INTERLEAVE = 4
CLASSES = (48, 64, 80, 96)
FAR = -1e30
VMEM_BYTES = 56 * 1024 * 1024
NT = (((1,), (1,)), ((), ()))


def vmem():
    return pl.BlockSpec(memory_space=pltpu.VMEM)


def smem():
    return pl.BlockSpec(memory_space=pltpu.SMEM)


def pack_pair(left, right, row_block, step):
    _, cols, width = left.shape
    heads = width // HEAD_DIM

    def body(left_ref, right_ref, out_ref):
        for i in range(step):
            for h in range(heads):
                at = slice(h * HEAD_DIM, (h + 1) * HEAD_DIM)
                out_ref[h, i] = jnp.concatenate([left_ref[i, :, at], right_ref[i, :, at]], axis=-1)

    count = len(row_block)

    def source(i):
        row = jnp.int32(row_block[0])
        for n in range(1, count):
            row = jnp.where(i == n, row_block[n], row)
        return (row, 0, 0)

    block = pl.BlockSpec((step, cols, width), source)
    return pl.pallas_call(
        body,
        grid=(count,),
        in_specs=[block, block],
        out_specs=pl.BlockSpec((heads, step, cols, 2 * HEAD_DIM), lambda i: (0, i, 0, 0)),
        out_shape=jax.ShapeDtypeStruct((heads, count * step, cols, 2 * HEAD_DIM), left.dtype),
    )(left, right)


def split_heads(in_ref, left_ref, right_ref):
    heads, step = in_ref.shape[:2]
    for i in range(step):
        for pair in range(heads // 2):
            first, second = in_ref[2 * pair, i], in_ref[2 * pair + 1, i]
            at = slice(pair * 2 * HEAD_DIM, (pair + 1) * 2 * HEAD_DIM)
            left_ref[i, :, at] = jnp.concatenate([first[:, :HEAD_DIM], second[:, :HEAD_DIM]], axis=1)
            right_ref[i, :, at] = jnp.concatenate([first[:, HEAD_DIM:], second[:, HEAD_DIM:]], axis=1)


def unpack_edge(packed, rows):
    heads, _, cols, lanes = packed.shape
    width = heads * HEAD_DIM
    out = pl.BlockSpec((HALO, cols, width), lambda i: (i * (rows // HALO - 1), 0, 0))
    shape = jax.ShapeDtypeStruct((rows, cols, width), packed.dtype)
    return pl.pallas_call(
        split_heads,
        grid=(2,),
        in_specs=[pl.BlockSpec((heads, HALO, cols, lanes), lambda i: (0, i, 0, 0))],
        out_specs=[out, out],
        out_shape=[shape, shape],
    )(packed)


def unpack_rest(packed, grad_queries, attended):
    heads, _, cols, lanes = packed.shape
    rows, _, width = attended.shape
    half = (rows - 2 * HALO) // HALO

    def body(in_ref, _, __, dq_ref, out_ref, dk_ref, dv_ref):
        step = pl.program_id(0)

        @pl.when(step < half)
        def _():
            split_heads(in_ref, dq_ref, out_ref)

        @pl.when(step >= half)
        def _():
            split_heads(in_ref, dk_ref, dv_ref)

    def query_row(i):
        return (jnp.minimum(i, half - 1) + 1, 0, 0)

    def key_row(i):
        mid = jnp.maximum(i, half) - half + 1
        return (jnp.where(i < 2 * half, mid, jnp.where(i == 2 * half, 0, half + 1)), 0, 0)

    shape = jax.ShapeDtypeStruct((rows, cols, width), packed.dtype)
    query_block = pl.BlockSpec((HALO, cols, width), query_row)
    key_block = pl.BlockSpec((HALO, cols, width), key_row)
    held = pl.BlockSpec(memory_space=pl.ANY)
    return pl.pallas_call(
        body,
        grid=(2 * half + 2,),
        in_specs=[pl.BlockSpec((heads, HALO, cols, lanes), lambda i: (0, i, 0, 0)), held, held],
        out_specs=[query_block, query_block, key_block, key_block],
        out_shape=[shape] * 4,
        input_output_aliases={1: 0, 2: 1},
    )(packed, grad_queries, attended)


def block_group(group, r, base, reach_class, w_first, w_last, kvw, kvt, qcw, dkv, sd, bias, qow):
    lanes = kvw.shape[-1]
    both = 2 * HALF
    scale = float(HEAD_DIM) ** -0.5
    lane = lax.broadcasted_iota(jnp.int32, (both, lanes), 1)
    off = REACH - reach_class
    width = HALF + 2 * reach_class
    taps = range(w_first, w_last)
    held = []
    for j in range(INTERLEAVE):
        block = group * INTERLEAVE + j
        start = pl.multiple_of(block * HALF, HALF)
        span = pl.ds(pl.multiple_of(start + off, 16), width)
        turned = pl.ds(pl.multiple_of(start - (j % 2) * HALF, both), WINDOW)
        rows_qc = jnp.concatenate(
            [qcw[r, pl.ds(start, HALF), :], qcw[r + 1, pl.ds(start, HALF), :]], axis=0)
        zero = jnp.zeros_like(rows_qc)
        qb = jnp.concatenate(
            [jnp.where(lane < HEAD_DIM, rows_qc * scale, zero),
             jnp.where(lane < HEAD_DIM, zero, rows_qc)], axis=0)
        held.append((start, span, turned, qb))
    tops = []
    for j in range(INTERLEAVE):
        _, span, _, qb = held[j]
        top = jnp.full((8, both), FAR, jnp.float32)
        for w in taps:
            product = lax.dot_general(kvw[base + w, span, :], qb, NT, preferred_element_type=jnp.float32)
            score = product[:, :both] + bias[w, off:off + width]
            sd[j, w, :width, :both] = score
            sd[j, w, :width, both:] = product[:, both:]
            top = jnp.maximum(top, jnp.max(score.reshape(width // 8, 8, both), axis=0))
        tops.append(jnp.max(top, axis=0, keepdims=True))
    sums = []
    for j in range(INTERLEAVE):
        total = jnp.zeros((8, both), jnp.float32)
        dot = jnp.zeros((8, both), jnp.float32)
        for w in taps:
            p = jnp.exp(sd[j, w, :width, :both] - tops[j])
            sd[j, w, :width, :both] = p
            total += jnp.sum(p.reshape(width // 8, 8, both), axis=0)
            dot += jnp.sum((p * sd[j, w, :width, both:]).reshape(width // 8, 8, both), axis=0)
        inverse = 1.0 / jnp.sum(total, axis=0, keepdims=True)
        sums.append((inverse, jnp.sum(dot, axis=0, keepdims=True) * inverse))
    edge = jnp.zeros((off, 2 * both), jnp.bfloat16)
    for j in range(INTERLEAVE):
        start, span, turned, qb = held[j]
        inverse, delta = sums[j]
        acc = jnp.zeros((lanes, 2 * both), jnp.float32)
        for w in taps:
            prob = sd[j, w, :width, :both] * inverse
            ds = (prob * (sd[j, w, :width, both:] - delta)).astype(jnp.bfloat16)
            dp = jnp.concatenate([ds, prob.astype(jnp.bfloat16)], axis=1)
            dkv[base + w, span, :] += jnp.dot(dp, qb, preferred_element_type=jnp.float32)
            if off:
                dp = jnp.concatenate([edge, dp, edge], axis=0)
            acc += jnp.dot(kvt[j % 2, base + w, :, turned], dp, preferred_element_type=jnp.float32)
        qo = jnp.concatenate([acc[:HEAD_DIM, :both] * scale, acc[HEAD_DIM:, both:]], axis=0)
        qo = qo.T.astype(jnp.bfloat16)
        qow[r, pl.ds(start, HALF), :] = qo[:HALF]
        qow[r + 1, pl.ds(start, HALF), :] = qo[HALF:]


def two_pairs(reach_ref, logw_ref, kvw, kvt, qcw, dkv, sd, bias, qow, key_stride, own_first, own_stride, ext_first,
              at_edge):
    blocks = qcw.shape[1] // HALF
    both = 2 * HALF

    @pl.loop(0, 2)
    def _(pair):
        base = pair * key_stride
        own = own_first + pair * own_stride
        r = 2 * pair
        key = lax.broadcasted_iota(jnp.int32, (WINDOW, both), 0) - REACH
        query = lax.broadcasted_iota(jnp.int32, (WINDOW, both), 1)
        second = query >= HALF
        gap = jnp.abs(key - jnp.where(second, query - HALF, query))
        near = gap <= jnp.where(second, reach_ref[own + 1], reach_ref[own])
        for w in range(TAPS):
            ok = near
            if w == 0:
                ok = near & jnp.logical_not(second)
            if w == TAPS - 1:
                ok = near & second
            bias[w] = jnp.where(ok, logw_ref[ext_first + base + w], FAR)

        widest = jnp.maximum(reach_ref[own], reach_ref[own + 1])

        def run(when, reach_class, w_first, w_last):
            @pl.when(when)
            def _():
                @pl.loop(0, blocks // INTERLEAVE)
                def _(group):
                    block_group(group, r, base, reach_class, w_first, w_last,
                                kvw, kvt, qcw, dkv, sd, bias, qow)

        rest = widest <= REACH
        if at_edge:
            no_above = logw_ref[ext_first + base + HALO - 1] < 0.5 * FAR
            no_below = logw_ref[ext_first + base + TAPS - HALO] < 0.5 * FAR
            run(no_above, REACH, HALO, TAPS)
            run(no_below, REACH, 0, TAPS - HALO)
            rest = jnp.logical_not(no_above | no_below)
        below = 0
        for reach_class in CLASSES:
            run(rest & (widest > below) & (widest <= reach_class), reach_class, 0, TAPS)
            below = reach_class


def wrap_and_turn(kvw, kvt):
    key_rows, padded, _ = kvw.shape
    ring = padded - 2 * REACH
    kvw[:, 0:REACH] = kvw[:, ring:ring + REACH]
    kvw[:, REACH + ring:padded] = kvw[:, REACH:2 * REACH]

    @pl.loop(0, key_rows)
    def _(kr):
        kvt[0, kr] = kvw[kr].T
        kvt[1, kr, :, 0:padded - HALF] = kvw[kr, HALF:].T


def fold(dkv):
    padded = dkv.shape[1]
    ring = padded - 2 * REACH
    dkv[:, ring:ring + REACH] += dkv[:, 0:REACH]
    dkv[:, REACH:2 * REACH] += dkv[:, REACH + ring:padded]


def scratch(key_rows, ring, lanes):
    padded = ring + 2 * REACH
    return [
        pltpu.VMEM((key_rows, padded, lanes), jnp.bfloat16),
        pltpu.VMEM((2, key_rows, lanes, padded), jnp.bfloat16),
        pltpu.VMEM((4, ring, lanes), jnp.bfloat16),
        pltpu.VMEM((key_rows, padded, lanes), jnp.float32),
        pltpu.VMEM((INTERLEAVE, TAPS, WINDOW, 4 * HALF), jnp.float32),
        pltpu.VMEM((TAPS, WINDOW, 2 * HALF), jnp.float32),
        pltpu.VMEM((4, ring, lanes), jnp.bfloat16),
    ]


def params():
    return pltpu.CompilerParams(vmem_limit_bytes=VMEM_BYTES)


def cost():
    return pl.CostEstimate(flops=20_000_000_000, bytes_accessed=8_000_000, transcendentals=5_000_000)


def attend_edge(reach, log_weight, kv, kv_above, kv_below, qc):
    sectors, rows, cols, lanes = kv.shape
    ring = sectors * cols
    ext_rows = rows + 2 * HALO

    def body(reach_ref, logw_ref, kv_ref, above_ref, below_ref, qc_ref, qo_ref, up_ref, down_ref, part_ref,
             kvw, kvt, qcw, dkv, sd, bias, qow):
        for s in range(sectors):
            at = slice(REACH + s * cols, REACH + (s + 1) * cols)
            kvw[0:HALO, at] = above_ref[s]
            kvw[HALO:HALO + rows, at] = kv_ref[s]
            kvw[HALO + rows:ext_rows, at] = below_ref[s]
            qcw[:, s * cols:(s + 1) * cols] = qc_ref[s]
        wrap_and_turn(kvw, kvt)

        @pl.loop(0, ext_rows)
        def _(kr):
            dkv[kr] = jnp.zeros(dkv.shape[1:], jnp.float32)

        two_pairs(reach_ref, logw_ref, kvw, kvt, qcw, dkv, sd, bias, qow,
                  rows - HALO, 0, rows - HALO, 0, True)
        fold(dkv)
        part_ref[...] = dkv[HALO:HALO + rows, REACH:REACH + ring]
        for s in range(sectors):
            at = slice(REACH + s * cols, REACH + (s + 1) * cols)
            qo_ref[s] = qow[:, s * cols:(s + 1) * cols]
            up_ref[s] = dkv[0:HALO, at].astype(jnp.bfloat16)
            down_ref[s] = dkv[rows + HALO:ext_rows, at].astype(jnp.bfloat16)

    def out(count):
        return jax.ShapeDtypeStruct((sectors, count, cols, lanes), jnp.bfloat16)

    return pl.pallas_call(
        body,
        in_specs=[smem(), smem(), vmem(), vmem(), vmem(), vmem()],
        out_specs=[vmem()] * 4,
        out_shape=[out(4), out(HALO), out(HALO), jax.ShapeDtypeStruct((rows, ring, lanes), jnp.float32)],
        scratch_shapes=scratch(ext_rows, ring, lanes),
        compiler_params=params(),
        cost_estimate=cost(),
    )(reach, log_weight, kv, kv_above, kv_below, qc)


def attend_mid(reach, log_weight, kv, qc, part):
    sectors, rows, cols, lanes = kv.shape
    ring = sectors * cols
    padded = ring + 2 * REACH

    def body(reach_ref, logw_ref, kv_ref, qc_ref, part_ref, out_ref, kvw, kvt, qcw, dkv, sd, bias, qow):
        for s in range(sectors):
            at = slice(REACH + s * cols, REACH + (s + 1) * cols)
            kvw[:, at] = kv_ref[s]
            qcw[:, s * cols:(s + 1) * cols] = qc_ref[s]
        wrap_and_turn(kvw, kvt)

        @pl.loop(0, rows)
        def _(kr):
            dkv[kr, 0:REACH] = jnp.zeros((REACH, lanes), jnp.float32)
            dkv[kr, REACH:REACH + ring] = part_ref[kr]
            dkv[kr, REACH + ring:padded] = jnp.zeros((REACH, lanes), jnp.float32)

        two_pairs(reach_ref, logw_ref, kvw, kvt, qcw, dkv, sd, bias, qow, HALO, HALO, HALO, HALO, False)
        fold(dkv)
        for s in range(sectors):
            at = slice(REACH + s * cols, REACH + (s + 1) * cols)
            out_ref[s, 0:4] = qow[:, s * cols:(s + 1) * cols]
            out_ref[s, 4:8] = dkv[HALO:rows - HALO, at].astype(jnp.bfloat16)
            out_ref[s, 8:10] = dkv[0:HALO, at].astype(jnp.bfloat16)
            out_ref[s, 10:12] = dkv[rows - HALO:rows, at].astype(jnp.bfloat16)

    return pl.pallas_call(
        body,
        in_specs=[smem(), smem(), vmem(), vmem(), vmem()],
        out_specs=vmem(),
        out_shape=jax.ShapeDtypeStruct((sectors, 12, cols, lanes), jnp.bfloat16),
        scratch_shapes=scratch(rows, ring, lanes),
        compiler_params=params(),
        cost_estimate=cost(),
    )(reach, log_weight, kv, qc, part)


def exchange(packed):
    return lax.all_to_all(packed, "lon", 0, 0)


def to_next_band(block, step):
    bands = lax.axis_size("lat")
    return lax.ppermute(block, "lat", [(i, i + step) for i in range(bands) if 0 <= i + step < bands])


def on_device(queries, key_vectors, value_vectors, cotangent, quad_weight, lon_reach):
    rows = queries.shape[0]
    ext = lax.axis_index("lat") * rows + jnp.arange(rows + 2 * HALO, dtype=jnp.int32) - HALO
    inside = (ext >= 0) & (ext < quad_weight.shape[0])
    log_weight = jnp.where(inside, jnp.log(quad_weight[jnp.clip(ext, 0, quad_weight.shape[0] - 1)]), FAR)

    kv = exchange(pack_pair(key_vectors, value_vectors, (0, 1), rows // 2))
    qc_edge = exchange(pack_pair(queries, cotangent, (0, rows // HALO - 1), HALO))
    above = to_next_band(kv[:, rows - HALO:], 1)
    below = to_next_band(kv[:, :HALO], -1)
    qc_mid, above, below = lax.optimization_barrier((pack_pair(queries, cotangent, (1, 2), HALO), above, below))
    qc_mid = exchange(qc_mid)
    qo_edge, up, down, part = attend_edge(lon_reach, log_weight, kv, above, below, qc_edge)
    from_below = to_next_band(up, -1)
    from_above = to_next_band(down, 1)
    grad_queries, attended = unpack_edge(exchange(qo_edge), rows)
    rest = attend_mid(lon_reach, log_weight, kv, qc_mid, part)
    home = jnp.concatenate([from_above, from_below], axis=1).astype(jnp.float32)
    edge = (rest[:, 8:].astype(jnp.float32) + home).astype(jnp.bfloat16)
    rest = exchange(lax.dynamic_update_slice(rest, edge, (0, 8, 0, 0)))
    grad_queries, attended, grad_keys, grad_values = unpack_rest(rest, grad_queries, attended)
    return attended, grad_queries, grad_keys, grad_values


def solution(mesh):
    cells = P("lat", "lon", None)
    return jax.shard_map(
        on_device,
        mesh=mesh,
        in_specs=(cells, cells, cells, cells, P(), P("lat")),
        out_specs=(cells, cells, cells, cells),
        check_vma=False,
    )
```

```python
import jax
import jax.numpy as jnp
from jax import lax
from jax.experimental import pallas as pl
from jax.experimental.pallas import tpu as pltpu
from jax.sharding import Mesh, PartitionSpec as P

HEADS = 16
HEAD_DIM = 64
HALO = 2
REACH = 96
HALF = 64
TAPS = 2 * HALO + 2
WINDOW = HALF + 2 * REACH
INTERLEAVE = 4
CLASSES = (48, 64, 80, 96)
FAR = -1e30
VMEM_BYTES = 56 * 1024 * 1024
NT = (((1,), (1,)), ((), ()))


def vmem():
    return pl.BlockSpec(memory_space=pltpu.VMEM)


def smem():
    return pl.BlockSpec(memory_space=pltpu.SMEM)


def pack_pair(left, right):
    rows, cols, width = left.shape
    heads = width // HEAD_DIM
    step = rows // 2

    def body(left_ref, right_ref, out_ref):
        for i in range(step):
            for h in range(heads):
                at = slice(h * HEAD_DIM, (h + 1) * HEAD_DIM)
                out_ref[h, i] = jnp.concatenate([left_ref[i, :, at], right_ref[i, :, at]], axis=-1)

    block = pl.BlockSpec((step, cols, width), lambda i: (i, 0, 0))
    return pl.pallas_call(
        body,
        grid=(2,),
        in_specs=[block, block],
        out_specs=pl.BlockSpec((heads, step, cols, 2 * HEAD_DIM), lambda i: (0, i, 0, 0)),
        out_shape=jax.ShapeDtypeStruct((heads, rows, cols, 2 * HEAD_DIM), left.dtype),
    )(left, right)


def unpack_pair(packed):
    heads, rows, cols, lanes = packed.shape
    width = heads * HEAD_DIM
    step = rows // 2

    def body(in_ref, left_ref, right_ref):
        for i in range(step):
            for pair in range(heads // 2):
                first, second = in_ref[2 * pair, i], in_ref[2 * pair + 1, i]
                at = slice(pair * 2 * HEAD_DIM, (pair + 1) * 2 * HEAD_DIM)
                left_ref[i, :, at] = jnp.concatenate([first[:, :HEAD_DIM], second[:, :HEAD_DIM]], axis=1)
                right_ref[i, :, at] = jnp.concatenate([first[:, HEAD_DIM:], second[:, HEAD_DIM:]], axis=1)

    out = pl.BlockSpec((step, cols, width), lambda i: (i, 0, 0))
    shape = jax.ShapeDtypeStruct((rows, cols, width), packed.dtype)
    return pl.pallas_call(
        body,
        grid=(2,),
        in_specs=[pl.BlockSpec((heads, step, cols, lanes), lambda i: (0, i, 0, 0))],
        out_specs=[out, out],
        out_shape=[shape, shape],
    )(packed)


def block_group(group, r, base, reach_class, w_first, w_last, kvw, kvt, qcw, dkv, sd, bias, qow):
    lanes = kvw.shape[-1]
    both = 2 * HALF
    scale = float(HEAD_DIM) ** -0.5
    lane = lax.broadcasted_iota(jnp.int32, (both, lanes), 1)
    off = REACH - reach_class
    width = HALF + 2 * reach_class
    taps = range(w_first, w_last)
    held = []
    for j in range(INTERLEAVE):
        block = group * INTERLEAVE + j
        start = pl.multiple_of(block * HALF, HALF)
        span = pl.ds(pl.multiple_of(start + off, 16), width)
        turned = pl.ds(pl.multiple_of(start - (j % 2) * HALF, both), WINDOW)
        rows_qc = jnp.concatenate(
            [qcw[r, pl.ds(start, HALF), :], qcw[r + 1, pl.ds(start, HALF), :]], axis=0)
        zero = jnp.zeros_like(rows_qc)
        qb = jnp.concatenate(
            [jnp.where(lane < HEAD_DIM, rows_qc * scale, zero),
             jnp.where(lane < HEAD_DIM, zero, rows_qc)], axis=0)
        held.append((start, span, turned, qb))
    tops = []
    for j in range(INTERLEAVE):
        _, span, _, qb = held[j]
        top = jnp.full((8, both), FAR, jnp.float32)
        for w in taps:
            product = lax.dot_general(kvw[base + w, span, :], qb, NT, preferred_element_type=jnp.float32)
            score = product[:, :both] + bias[w, off:off + width]
            sd[j, w, :width, :both] = score
            sd[j, w, :width, both:] = product[:, both:]
            top = jnp.maximum(top, jnp.max(score.reshape(width // 8, 8, both), axis=0))
        tops.append(jnp.max(top, axis=0, keepdims=True))
    sums = []
    for j in range(INTERLEAVE):
        total = jnp.zeros((8, both), jnp.float32)
        dot = jnp.zeros((8, both), jnp.float32)
        for w in taps:
            p = jnp.exp(sd[j, w, :width, :both] - tops[j])
            sd[j, w, :width, :both] = p
            total += jnp.sum(p.reshape(width // 8, 8, both), axis=0)
            dot += jnp.sum((p * sd[j, w, :width, both:]).reshape(width // 8, 8, both), axis=0)
        inverse = 1.0 / jnp.sum(total, axis=0, keepdims=True)
        sums.append((inverse, jnp.sum(dot, axis=0, keepdims=True) * inverse))
    edge = jnp.zeros((off, 2 * both), jnp.bfloat16)
    for j in range(INTERLEAVE):
        start, span, turned, qb = held[j]
        inverse, delta = sums[j]
        acc = jnp.zeros((lanes, 2 * both), jnp.float32)
        for w in taps:
            prob = sd[j, w, :width, :both] * inverse
            ds = (prob * (sd[j, w, :width, both:] - delta)).astype(jnp.bfloat16)
            dp = jnp.concatenate([ds, prob.astype(jnp.bfloat16)], axis=1)
            dkv[base + w, span, :] += jnp.dot(dp, qb, preferred_element_type=jnp.float32)
            if off:
                dp = jnp.concatenate([edge, dp, edge], axis=0)
            acc += jnp.dot(kvt[j % 2, base + w, :, turned], dp, preferred_element_type=jnp.float32)
        qo = jnp.concatenate([acc[:HEAD_DIM, :both] * scale, acc[HEAD_DIM:, both:]], axis=0)
        qo = qo.T.astype(jnp.bfloat16)
        qow[r, pl.ds(start, HALF), :] = qo[:HALF]
        qow[r + 1, pl.ds(start, HALF), :] = qo[HALF:]


def row_pairs(reach_ref, logw_ref, kvw, kvt, qcw, dkv, sd, bias, qow):
    blocks = qcw.shape[1] // HALF
    both = 2 * HALF

    @pl.loop(0, 4)
    def _(pair):
        r = 2 * pair
        base = r + jnp.where(pair >= 2, 2 * HALO, 0)
        key = lax.broadcasted_iota(jnp.int32, (WINDOW, both), 0) - REACH
        query = lax.broadcasted_iota(jnp.int32, (WINDOW, both), 1)
        second = query >= HALF
        gap = jnp.abs(key - jnp.where(second, query - HALF, query))
        near = gap <= jnp.where(second, reach_ref[r + 1], reach_ref[r])
        for w in range(TAPS):
            ok = near
            if w == 0:
                ok = near & jnp.logical_not(second)
            if w == TAPS - 1:
                ok = near & second
            bias[w] = jnp.where(ok, logw_ref[base + w], FAR)

        widest = jnp.maximum(reach_ref[r], reach_ref[r + 1])

        def run(when, reach_class, w_first, w_last):
            @pl.when(when)
            def _():
                @pl.loop(0, blocks // INTERLEAVE)
                def _(group):
                    block_group(group, r, base, reach_class, w_first, w_last,
                                kvw, kvt, qcw, dkv, sd, bias, qow)

        no_above = logw_ref[base + HALO - 1] < 0.5 * FAR
        no_below = logw_ref[base + TAPS - HALO] < 0.5 * FAR
        run(no_above, REACH, HALO, TAPS)
        run(no_below, REACH, 0, TAPS - HALO)
        rest = jnp.logical_not(no_above | no_below)
        below = 0
        for reach_class in CLASSES:
            run(rest & (widest > below) & (widest <= reach_class), reach_class, 0, TAPS)
            below = reach_class


def attend(second_half, reach, log_weight, kv, kv_partner, kv_plane, qc):
    _, sectors, rows, cols, lanes = kv.shape
    ring = sectors * cols
    padded = ring + 2 * REACH
    run = rows + 2 * HALO

    def body(half_ref, reach_ref, logw_ref, kv_ref, partner_ref, plane_ref, qc_ref,
             qo_ref, own_ref, to_partner_ref, to_plane_ref, kvw, kvt, qcw, dkv, sd, bias, qow):
        first = half_ref[0] == 0
        for s in range(sectors):
            at = slice(REACH + s * cols, REACH + (s + 1) * cols)
            for n in range(2):
                kvw[n * run + HALO:n * run + HALO + rows, at] = kv_ref[n, s]
                qcw[n * rows:(n + 1) * rows, s * cols:(s + 1) * cols] = qc_ref[n, s]

        @pl.when(first)
        def _():
            for s in range(sectors):
                at = slice(REACH + s * cols, REACH + (s + 1) * cols)
                kvw[0:2, at] = plane_ref[s]
                kvw[6:8, at] = partner_ref[0, s, 0:2]
                kvw[8:10, at] = partner_ref[0, s, 2:4]
                kvw[14:16, at] = partner_ref[1, s, 0:2]

        @pl.when(jnp.logical_not(first))
        def _():
            for s in range(sectors):
                at = slice(REACH + s * cols, REACH + (s + 1) * cols)
                kvw[0:2, at] = partner_ref[0, s, 2:4]
                kvw[6:8, at] = partner_ref[1, s, 0:2]
                kvw[8:10, at] = partner_ref[1, s, 2:4]
                kvw[14:16, at] = plane_ref[s]

        kvw[:, 0:REACH] = kvw[:, ring:ring + REACH]
        kvw[:, REACH + ring:padded] = kvw[:, REACH:2 * REACH]

        @pl.loop(0, 2 * run)
        def _(kr):
            kvt[0, kr] = kvw[kr].T
            kvt[1, kr, :, 0:padded - HALF] = kvw[kr, HALF:].T
            dkv[kr] = jnp.zeros((padded, lanes), jnp.float32)

        row_pairs(reach_ref, logw_ref, kvw, kvt, qcw, dkv, sd, bias, qow)

        dkv[:, ring:ring + REACH] += dkv[:, 0:REACH]
        dkv[:, REACH:2 * REACH] += dkv[:, REACH + ring:padded]
        for s in range(sectors):
            at = slice(REACH + s * cols, REACH + (s + 1) * cols)
            for n in range(2):
                qo_ref[n, s] = qow[n * rows:(n + 1) * rows, s * cols:(s + 1) * cols]
                own_ref[n, s] = dkv[n * run + HALO:n * run + HALO + rows, at].astype(jnp.bfloat16)

        @pl.when(first)
        def _():
            for s in range(sectors):
                at = slice(REACH + s * cols, REACH + (s + 1) * cols)
                to_partner_ref[s, 0:4] = dkv[6:10, at].astype(jnp.bfloat16)
                to_partner_ref[s, 4:6] = dkv[14:16, at].astype(jnp.bfloat16)
                to_plane_ref[s] = dkv[0:2, at].astype(jnp.bfloat16)

        @pl.when(jnp.logical_not(first))
        def _():
            for s in range(sectors):
                at = slice(REACH + s * cols, REACH + (s + 1) * cols)
                to_partner_ref[s, 0:2] = dkv[0:2, at].astype(jnp.bfloat16)
                to_partner_ref[s, 2:6] = dkv[6:10, at].astype(jnp.bfloat16)
                to_plane_ref[s] = dkv[14:16, at].astype(jnp.bfloat16)

    whole = jax.ShapeDtypeStruct(kv.shape, jnp.bfloat16)

    def out(count):
        return jax.ShapeDtypeStruct((sectors, count, cols, lanes), jnp.bfloat16)

    return pl.pallas_call(
        body,
        in_specs=[smem(), smem(), smem(), vmem(), vmem(), vmem(), vmem()],
        out_specs=[vmem()] * 4,
        out_shape=[whole, whole, out(3 * HALO), out(HALO)],
        scratch_shapes=[
            pltpu.VMEM((2 * run, padded, lanes), jnp.bfloat16),
            pltpu.VMEM((2, 2 * run, lanes, padded), jnp.bfloat16),
            pltpu.VMEM((2 * rows, ring, lanes), jnp.bfloat16),
            pltpu.VMEM((2 * run, padded, lanes), jnp.float32),
            pltpu.VMEM((INTERLEAVE, TAPS, WINDOW, 4 * HALF), jnp.float32),
            pltpu.VMEM((TAPS, WINDOW, 2 * HALF), jnp.float32),
            pltpu.VMEM((2 * rows, ring, lanes), jnp.bfloat16),
        ],
        compiler_params=pltpu.CompilerParams(vmem_limit_bytes=VMEM_BYTES),
        cost_estimate=pl.CostEstimate(flops=40_000_000_000, bytes_accessed=10_000_000, transcendentals=5_000_000),
    )(second_half, reach, log_weight, kv, kv_partner, kv_plane, qc)


def add_home(second_half, own, partner, plane):
    runs, sectors, rows, cols, lanes = own.shape
    step = sectors // 4

    def body(half_ref, own_ref, partner_ref, plane_ref, out_ref):
        def add(order):
            for n, (ref, row) in enumerate(order):
                at = slice((n % 2) * HALO, (n % 2 + 1) * HALO)
                other = ref[:, row:row + HALO].astype(jnp.float32)
                out_ref[n // 2, :, at] = (own_ref[n // 2, :, at].astype(jnp.float32) + other).astype(out_ref.dtype)

        @pl.when(half_ref[0] == 0)
        def _():
            add([(plane_ref, 0), (partner_ref, 0), (partner_ref, 2), (partner_ref, 4)])

        @pl.when(half_ref[0] != 0)
        def _():
            add([(partner_ref, 0), (partner_ref, 2), (partner_ref, 4), (plane_ref, 0)])

    block = pl.BlockSpec((runs, step, rows, cols, lanes), lambda i: (0, i, 0, 0, 0))

    def side(count):
        return pl.BlockSpec((step, count, cols, lanes), lambda i: (i, 0, 0, 0))

    return pl.pallas_call(
        body,
        grid=(4,),
        in_specs=[smem(), block, side(3 * HALO), side(HALO)],
        out_specs=block,
        out_shape=jax.ShapeDtypeStruct(own.shape, own.dtype),
    )(second_half, own, partner, plane)


def exchange(packed):
    return lax.all_to_all(packed, ("band", "lon"), 0, 0)


def to_partner(block):
    return lax.ppermute(block, "lon", [(i, i ^ 1) for i in range(lax.axis_size("lon"))])


def to_next_plane(block):
    planes, columns = lax.axis_size("plane"), lax.axis_size("lon")
    route = []
    for plane in range(planes - 1):
        for i in range(1, columns, 2):
            here, there = plane * columns + i, (plane + 1) * columns + i - 1
            route += [(here, there), (there, here)]
    return lax.ppermute(block, ("plane", "lon"), route)


def on_device(queries, key_vectors, value_vectors, cotangent, quad_weight, lon_reach):
    rows, cols, _ = queries.shape
    half_rows = rows // 2
    bands, sectors = lax.axis_size("band"), lax.axis_size("lon")
    half = lax.axis_index("lon") % 2
    parted = (bands * sectors, half_rows, cols, 2 * HEAD_DIM)
    by_band = (bands, sectors, half_rows, cols, 2 * HEAD_DIM)

    other_reach = lax.ppermute(lon_reach, "band", [(0, 1), (1, 0)])
    lower = lax.axis_index("band") == 0
    reach = jnp.stack([jnp.where(lower, lon_reach, other_reach), jnp.where(lower, other_reach, lon_reach)])
    reach = lax.dynamic_slice_in_dim(reach, half * half_rows, half_rows, axis=1).reshape(-1)
    ext = (lax.axis_index("plane") * bands + jnp.arange(bands)[:, None]) * rows + half * half_rows - HALO
    ext = (ext + jnp.arange(half_rows + 2 * HALO)[None, :]).reshape(-1)
    inside = (ext >= 0) & (ext < quad_weight.shape[0])
    log_weight = jnp.where(inside, jnp.log(quad_weight[jnp.clip(ext, 0, quad_weight.shape[0] - 1)]), FAR)
    second_half = half.astype(jnp.int32).reshape(1)

    kv = exchange(pack_pair(key_vectors, value_vectors).reshape(parted)).reshape(by_band)
    rim = jnp.where(half == 0, kv[0, :, :HALO], kv[1, :, half_rows - HALO:])
    kv_plane = to_next_plane(rim)
    kv_partner = to_partner(kv)
    qc = exchange(pack_pair(queries, cotangent).reshape(parted)).reshape(by_band)
    qo, own, partner, plane = attend(second_half, reach, log_weight, kv, kv_partner, kv_plane, qc)
    plane = to_next_plane(plane)
    partner = to_partner(partner)
    packed = (HEADS, rows, cols, 2 * HEAD_DIM)
    grad_queries, attended = unpack_pair(exchange(qo.reshape(parted)).reshape(packed))
    total = add_home(second_half, own, partner, plane)
    grad_keys, grad_values = unpack_pair(exchange(total.reshape(parted)).reshape(packed))
    return attended, grad_queries, grad_keys, grad_values


def solution(mesh):
    bands, sectors = mesh.devices.shape
    planes = Mesh(mesh.devices.reshape(bands // 2, 2, sectors), ("plane", "band", "lon"))
    cells = P(("plane", "band"), "lon", None)
    return jax.shard_map(
        on_device,
        mesh=planes,
        in_specs=(cells, cells, cells, cells, P(), P(("plane", "band"))),
        out_specs=(cells, cells, cells, cells),
        check_vma=False,
    )
```

```python
import jax
import jax.numpy as jnp
from jax import lax
from jax.experimental import pallas as pl
from jax.experimental.pallas import tpu as pltpu
from jax.sharding import Mesh, PartitionSpec as P

HEADS = 16
HEAD_DIM = 64
HALO = 2
REACH = 96
HALF = 64
TAPS = 2 * HALO + 2
WINDOW = HALF + 2 * REACH
INTERLEAVE = 6
CLASSES = (48, 64, 80, 96)
FAR = -1e30
VMEM_BYTES = 60 * 1024 * 1024
SMALL_BYTES = 8 * 1024 * 1024
NT = (((1,), (1,)), ((), ()))


def vmem():
    return pl.BlockSpec(memory_space=pltpu.VMEM)


def smem():
    return pl.BlockSpec(memory_space=pltpu.SMEM)


def params(limit):
    return pltpu.CompilerParams(vmem_limit_bytes=limit)


def pack_pair(left, right):
    rows, cols, width = left.shape
    heads = width // HEAD_DIM
    step = rows // 2

    def body(left_ref, right_ref, out_ref):
        for i in range(step):
            for h in range(heads):
                at = slice(h * HEAD_DIM, (h + 1) * HEAD_DIM)
                out_ref[h, i] = jnp.concatenate([left_ref[i, :, at], right_ref[i, :, at]], axis=-1)

    block = pl.BlockSpec((step, cols, width), lambda i: (i, 0, 0))
    return pl.pallas_call(
        body,
        grid=(2,),
        in_specs=[block, block],
        out_specs=pl.BlockSpec((heads, step, cols, 2 * HEAD_DIM), lambda i: (0, i, 0, 0)),
        out_shape=jax.ShapeDtypeStruct((heads, rows, cols, 2 * HEAD_DIM), left.dtype),
        compiler_params=params(SMALL_BYTES),
    )(left, right)


def unpack_pair(packed):
    heads, rows, cols, lanes = packed.shape
    width = heads * HEAD_DIM
    step = rows // 2

    def body(in_ref, left_ref, right_ref):
        for i in range(step):
            for pair in range(heads // 2):
                first, second = in_ref[2 * pair, i], in_ref[2 * pair + 1, i]
                at = slice(pair * 2 * HEAD_DIM, (pair + 1) * 2 * HEAD_DIM)
                left_ref[i, :, at] = jnp.concatenate([first[:, :HEAD_DIM], second[:, :HEAD_DIM]], axis=1)
                right_ref[i, :, at] = jnp.concatenate([first[:, HEAD_DIM:], second[:, HEAD_DIM:]], axis=1)

    out = pl.BlockSpec((step, cols, width), lambda i: (i, 0, 0))
    shape = jax.ShapeDtypeStruct((rows, cols, width), packed.dtype)
    return pl.pallas_call(
        body,
        grid=(2,),
        in_specs=[pl.BlockSpec((heads, step, cols, lanes), lambda i: (0, i, 0, 0))],
        out_specs=[out, out],
        out_shape=[shape, shape],
        compiler_params=params(SMALL_BYTES),
    )(packed)


def block_group(group, r, base, reach_class, w_first, w_last, kvw, kvt, qcw, dkv, sd, bias, qow):
    lanes = kvw.shape[-1]
    both = 2 * HALF
    scale = float(HEAD_DIM) ** -0.5
    lane = lax.broadcasted_iota(jnp.int32, (both, lanes), 1)
    off = REACH - reach_class
    width = HALF + 2 * reach_class
    taps = range(w_first, w_last)
    held = []
    for j in range(INTERLEAVE):
        block = group * INTERLEAVE + j
        start = pl.multiple_of(block * HALF, HALF)
        span = pl.ds(pl.multiple_of(start + off, 16), width)
        turned = pl.ds(pl.multiple_of(start - (j % 2) * HALF, both), WINDOW)
        rows_qc = jnp.concatenate(
            [qcw[r, pl.ds(start, HALF), :], qcw[r + 1, pl.ds(start, HALF), :]], axis=0)
        zero = jnp.zeros_like(rows_qc)
        qb = jnp.concatenate(
            [jnp.where(lane < HEAD_DIM, rows_qc * scale, zero),
             jnp.where(lane < HEAD_DIM, zero, rows_qc)], axis=0)
        held.append((start, span, turned, qb))
    tops = []
    for j in range(INTERLEAVE):
        _, span, _, qb = held[j]
        top = jnp.full((8, both), FAR, jnp.float32)
        for w in taps:
            product = lax.dot_general(kvw[base + w, span, :], qb, NT, preferred_element_type=jnp.float32)
            score = product[:, :both] + bias[w, off:off + width]
            sd[j, w, :width, :both] = score
            sd[j, w, :width, both:] = product[:, both:]
            top = jnp.maximum(top, jnp.max(score.reshape(width // 8, 8, both), axis=0))
        tops.append(jnp.max(top, axis=0, keepdims=True))
    sums = []
    for j in range(INTERLEAVE):
        total = jnp.zeros((8, both), jnp.float32)
        dot = jnp.zeros((8, both), jnp.float32)
        for w in taps:
            p = jnp.exp(sd[j, w, :width, :both] - tops[j])
            sd[j, w, :width, :both] = p
            total += jnp.sum(p.reshape(width // 8, 8, both), axis=0)
            dot += jnp.sum((p * sd[j, w, :width, both:]).reshape(width // 8, 8, both), axis=0)
        inverse = 1.0 / jnp.sum(total, axis=0, keepdims=True)
        sums.append((inverse, jnp.sum(dot, axis=0, keepdims=True) * inverse))
    edge = jnp.zeros((off, 2 * both), jnp.bfloat16)
    for j in range(INTERLEAVE):
        start, span, turned, qb = held[j]
        inverse, delta = sums[j]
        acc = jnp.zeros((lanes, 2 * both), jnp.float32)
        for w in taps:
            prob = sd[j, w, :width, :both] * inverse
            ds = (prob * (sd[j, w, :width, both:] - delta)).astype(jnp.bfloat16)
            dp = jnp.concatenate([ds, prob.astype(jnp.bfloat16)], axis=1)
            dkv[base + w, span, :] += jnp.dot(dp, qb, preferred_element_type=jnp.float32)
            if off:
                dp = jnp.concatenate([edge, dp, edge], axis=0)
            acc += jnp.dot(kvt[j % 2, base + w, :, turned], dp, preferred_element_type=jnp.float32)
        qo = jnp.concatenate([acc[:HEAD_DIM, :both] * scale, acc[HEAD_DIM:, both:]], axis=0)
        qo = qo.T.astype(jnp.bfloat16)
        qow[r, pl.ds(start, HALF), :] = qo[:HALF]
        qow[r + 1, pl.ds(start, HALF), :] = qo[HALF:]


def row_pairs(reach_ref, logw_ref, kvw, kvt, qcw, dkv, sd, bias, qow):
    blocks = qcw.shape[1] // HALF
    both = 2 * HALF

    @pl.loop(0, 4)
    def _(pair):
        r = 2 * pair
        base = r + jnp.where(pair >= 2, 2 * HALO, 0)
        key = lax.broadcasted_iota(jnp.int32, (WINDOW, both), 0) - REACH
        query = lax.broadcasted_iota(jnp.int32, (WINDOW, both), 1)
        second = query >= HALF
        gap = jnp.abs(key - jnp.where(second, query - HALF, query))
        near = gap <= jnp.where(second, reach_ref[r + 1], reach_ref[r])
        for w in range(TAPS):
            ok = near
            if w == 0:
                ok = near & jnp.logical_not(second)
            if w == TAPS - 1:
                ok = near & second
            bias[w] = jnp.where(ok, logw_ref[base + w], FAR)

        widest = jnp.maximum(reach_ref[r], reach_ref[r + 1])

        def run(when, reach_class, w_first, w_last):
            @pl.when(when)
            def _():
                @pl.loop(0, blocks // INTERLEAVE)
                def _(group):
                    block_group(group, r, base, reach_class, w_first, w_last,
                                kvw, kvt, qcw, dkv, sd, bias, qow)

        no_above = logw_ref[base + HALO - 1] < 0.5 * FAR
        no_below = logw_ref[base + TAPS - HALO] < 0.5 * FAR
        run(no_above, REACH, HALO, TAPS)
        run(no_below, REACH, 0, TAPS - HALO)
        rest = jnp.logical_not(no_above | no_below)
        below = 0
        for reach_class in CLASSES:
            run(rest & (widest > below) & (widest <= reach_class), reach_class, 0, TAPS)
            below = reach_class


def attend(second_half, reach, log_weight, kv, kv_partner, kv_plane, qc):
    _, sectors, rows, cols, lanes = kv.shape
    ring = sectors * cols
    padded = ring + 2 * REACH
    run = rows + 2 * HALO

    def body(half_ref, reach_ref, logw_ref, kv_ref, partner_ref, plane_ref, qc_ref,
             qo_ref, own_ref, to_partner_ref, to_plane_ref, kvw, kvt, qcw, dkv, sd, bias, qow):
        first = half_ref[0] == 0
        for s in range(sectors):
            at = slice(REACH + s * cols, REACH + (s + 1) * cols)
            for n in range(2):
                kvw[n * run + HALO:n * run + HALO + rows, at] = kv_ref[n, s]
                qcw[n * rows:(n + 1) * rows, s * cols:(s + 1) * cols] = qc_ref[n, s]

        @pl.when(first)
        def _():
            for s in range(sectors):
                at = slice(REACH + s * cols, REACH + (s + 1) * cols)
                kvw[0:2, at] = plane_ref[s]
                kvw[6:8, at] = partner_ref[0, s, 0:2]
                kvw[8:10, at] = partner_ref[0, s, 2:4]
                kvw[14:16, at] = partner_ref[1, s, 0:2]

        @pl.when(jnp.logical_not(first))
        def _():
            for s in range(sectors):
                at = slice(REACH + s * cols, REACH + (s + 1) * cols)
                kvw[0:2, at] = partner_ref[0, s, 2:4]
                kvw[6:8, at] = partner_ref[1, s, 0:2]
                kvw[8:10, at] = partner_ref[1, s, 2:4]
                kvw[14:16, at] = plane_ref[s]

        kvw[:, 0:REACH] = kvw[:, ring:ring + REACH]
        kvw[:, REACH + ring:padded] = kvw[:, REACH:2 * REACH]

        @pl.loop(0, 2 * run)
        def _(kr):
            kvt[0, kr] = kvw[kr].T
            kvt[1, kr, :, 0:padded - HALF] = kvw[kr, HALF:].T
            dkv[kr] = jnp.zeros((padded, lanes), jnp.float32)

        row_pairs(reach_ref, logw_ref, kvw, kvt, qcw, dkv, sd, bias, qow)

        dkv[:, ring:ring + REACH] += dkv[:, 0:REACH]
        dkv[:, REACH:2 * REACH] += dkv[:, REACH + ring:padded]
        for s in range(sectors):
            at = slice(REACH + s * cols, REACH + (s + 1) * cols)
            for n in range(2):
                qo_ref[n, s] = qow[n * rows:(n + 1) * rows, s * cols:(s + 1) * cols]
                own_ref[n, s] = dkv[n * run + HALO:n * run + HALO + rows, at].astype(jnp.bfloat16)

        @pl.when(first)
        def _():
            for s in range(sectors):
                at = slice(REACH + s * cols, REACH + (s + 1) * cols)
                to_partner_ref[s, 0:4] = dkv[6:10, at].astype(jnp.bfloat16)
                to_partner_ref[s, 4:6] = dkv[14:16, at].astype(jnp.bfloat16)
                to_plane_ref[s] = dkv[0:2, at].astype(jnp.bfloat16)

        @pl.when(jnp.logical_not(first))
        def _():
            for s in range(sectors):
                at = slice(REACH + s * cols, REACH + (s + 1) * cols)
                to_partner_ref[s, 0:2] = dkv[0:2, at].astype(jnp.bfloat16)
                to_partner_ref[s, 2:6] = dkv[6:10, at].astype(jnp.bfloat16)
                to_plane_ref[s] = dkv[14:16, at].astype(jnp.bfloat16)

    whole = jax.ShapeDtypeStruct(kv.shape, jnp.bfloat16)

    def out(count):
        return jax.ShapeDtypeStruct((sectors, count, cols, lanes), jnp.bfloat16)

    return pl.pallas_call(
        body,
        in_specs=[smem(), smem(), smem(), vmem(), vmem(), vmem(), vmem()],
        out_specs=[vmem()] * 4,
        out_shape=[whole, whole, out(3 * HALO), out(HALO)],
        scratch_shapes=[
            pltpu.VMEM((2 * run, padded, lanes), jnp.bfloat16),
            pltpu.VMEM((2, 2 * run, lanes, padded), jnp.bfloat16),
            pltpu.VMEM((2 * rows, ring, lanes), jnp.bfloat16),
            pltpu.VMEM((2 * run, padded, lanes), jnp.float32),
            pltpu.VMEM((INTERLEAVE, TAPS, WINDOW, 4 * HALF), jnp.float32),
            pltpu.VMEM((TAPS, WINDOW, 2 * HALF), jnp.float32),
            pltpu.VMEM((2 * rows, ring, lanes), jnp.bfloat16),
        ],
        compiler_params=params(VMEM_BYTES),
        cost_estimate=pl.CostEstimate(flops=40_000_000_000, bytes_accessed=10_000_000, transcendentals=5_000_000),
    )(second_half, reach, log_weight, kv, kv_partner, kv_plane, qc)


def add_home(second_half, own, partner, plane):
    runs, sectors, rows, cols, lanes = own.shape
    step = sectors // 4

    def body(half_ref, own_ref, partner_ref, plane_ref, out_ref):
        def add(order):
            for n, (ref, row) in enumerate(order):
                at = slice((n % 2) * HALO, (n % 2 + 1) * HALO)
                other = ref[:, row:row + HALO].astype(jnp.float32)
                out_ref[n // 2, :, at] = (own_ref[n // 2, :, at].astype(jnp.float32) + other).astype(out_ref.dtype)

        @pl.when(half_ref[0] == 0)
        def _():
            add([(plane_ref, 0), (partner_ref, 0), (partner_ref, 2), (partner_ref, 4)])

        @pl.when(half_ref[0] != 0)
        def _():
            add([(partner_ref, 0), (partner_ref, 2), (partner_ref, 4), (plane_ref, 0)])

    block = pl.BlockSpec((runs, step, rows, cols, lanes), lambda i: (0, i, 0, 0, 0))

    def side(count):
        return pl.BlockSpec((step, count, cols, lanes), lambda i: (i, 0, 0, 0))

    return pl.pallas_call(
        body,
        grid=(4,),
        in_specs=[smem(), block, side(3 * HALO), side(HALO)],
        out_specs=block,
        out_shape=jax.ShapeDtypeStruct(own.shape, own.dtype),
        compiler_params=params(SMALL_BYTES),
    )(second_half, own, partner, plane)


def exchange(packed):
    return lax.all_to_all(packed, ("band", "lon"), 0, 0)


def to_partner(block):
    return lax.ppermute(block, "lon", [(i, i ^ 1) for i in range(lax.axis_size("lon"))])


def to_next_plane(block):
    planes, columns = lax.axis_size("plane"), lax.axis_size("lon")
    route = []
    for plane in range(planes - 1):
        for i in range(1, columns, 2):
            here, there = plane * columns + i, (plane + 1) * columns + i - 1
            route += [(here, there), (there, here)]
    return lax.ppermute(block, ("plane", "lon"), route)


def on_device(queries, key_vectors, value_vectors, cotangent, quad_weight, lon_reach):
    rows, cols, _ = queries.shape
    half_rows = rows // 2
    bands, sectors = lax.axis_size("band"), lax.axis_size("lon")
    half = lax.axis_index("lon") % 2
    parted = (bands * sectors, half_rows, cols, 2 * HEAD_DIM)
    by_band = (bands, sectors, half_rows, cols, 2 * HEAD_DIM)

    other_reach = lax.ppermute(lon_reach, "band", [(0, 1), (1, 0)])
    lower = lax.axis_index("band") == 0
    reach = jnp.stack([jnp.where(lower, lon_reach, other_reach), jnp.where(lower, other_reach, lon_reach)])
    reach = lax.dynamic_slice_in_dim(reach, half * half_rows, half_rows, axis=1).reshape(-1)
    ext = (lax.axis_index("plane") * bands + jnp.arange(bands)[:, None]) * rows + half * half_rows - HALO
    ext = (ext + jnp.arange(half_rows + 2 * HALO)[None, :]).reshape(-1)
    inside = (ext >= 0) & (ext < quad_weight.shape[0])
    log_weight = jnp.where(inside, jnp.log(quad_weight[jnp.clip(ext, 0, quad_weight.shape[0] - 1)]), FAR)
    second_half = half.astype(jnp.int32).reshape(1)

    kv = exchange(pack_pair(key_vectors, value_vectors).reshape(parted)).reshape(by_band)
    rim = jnp.where(half == 0, kv[0, :, :HALO], kv[1, :, half_rows - HALO:])
    kv_plane = to_next_plane(rim)
    kv_partner = to_partner(kv)
    qc = exchange(pack_pair(queries, cotangent).reshape(parted)).reshape(by_band)
    qo, own, partner, plane = attend(second_half, reach, log_weight, kv, kv_partner, kv_plane, qc)
    plane = to_next_plane(plane)
    partner = to_partner(partner)
    packed = (HEADS, rows, cols, 2 * HEAD_DIM)
    grad_queries, attended = unpack_pair(exchange(qo.reshape(parted)).reshape(packed))
    total = add_home(second_half, own, partner, plane)
    grad_keys, grad_values = unpack_pair(exchange(total.reshape(parted)).reshape(packed))
    return attended, grad_queries, grad_keys, grad_values


def solution(mesh):
    bands, sectors = mesh.devices.shape
    planes = Mesh(mesh.devices.reshape(bands // 2, 2, sectors), ("plane", "band", "lon"))
    cells = P(("plane", "band"), "lon", None)
    return jax.shard_map(
        on_device,
        mesh=planes,
        in_specs=(cells, cells, cells, cells, P(), P(("plane", "band"))),
        out_specs=(cells, cells, cells, cells),
        check_vma=False,
    )
```

```python
import jax
import jax.numpy as jnp
from jax import lax
from jax.experimental import pallas as pl
from jax.experimental.pallas import tpu as pltpu
from jax.sharding import Mesh, PartitionSpec as P

HEADS = 16
HEAD_DIM = 64
HALO = 2
REACH = 96
HALF = 64
TAPS = 2 * HALO + 2
WINDOW = HALF + 2 * REACH
INTERLEAVE = 6
CLASSES = (48, 64, 80, 96)
FAR = -1e30
VMEM_BYTES = 52 * 1024 * 1024
SMALL_BYTES = 8 * 1024 * 1024
LARGE_BYTES = 60 * 1024 * 1024
NT = (((1,), (1,)), ((), ()))


def vmem():
    return pl.BlockSpec(memory_space=pltpu.VMEM)


def smem():
    return pl.BlockSpec(memory_space=pltpu.SMEM)


def params(limit):
    return pltpu.CompilerParams(vmem_limit_bytes=limit)


def pack_pair(left, right):
    rows, cols, width = left.shape
    heads = width // HEAD_DIM
    step = rows // 2

    def body(left_ref, right_ref, out_ref):
        for i in range(step):
            for h in range(heads):
                at = slice(h * HEAD_DIM, (h + 1) * HEAD_DIM)
                out_ref[h, i] = jnp.concatenate([left_ref[i, :, at], right_ref[i, :, at]], axis=-1)

    block = pl.BlockSpec((step, cols, width), lambda i: (i, 0, 0))
    return pl.pallas_call(
        body,
        grid=(2,),
        in_specs=[block, block],
        out_specs=pl.BlockSpec((heads, step, cols, 2 * HEAD_DIM), lambda i: (0, i, 0, 0)),
        out_shape=jax.ShapeDtypeStruct((heads, rows, cols, 2 * HEAD_DIM), left.dtype),
        compiler_params=params(LARGE_BYTES),
    )(left, right)


def unpack_pair(packed):
    heads, rows, cols, lanes = packed.shape
    width = heads * HEAD_DIM
    step = rows // 2

    def body(in_ref, left_ref, right_ref):
        for i in range(step):
            for pair in range(heads // 2):
                first, second = in_ref[2 * pair, i], in_ref[2 * pair + 1, i]
                at = slice(pair * 2 * HEAD_DIM, (pair + 1) * 2 * HEAD_DIM)
                left_ref[i, :, at] = jnp.concatenate([first[:, :HEAD_DIM], second[:, :HEAD_DIM]], axis=1)
                right_ref[i, :, at] = jnp.concatenate([first[:, HEAD_DIM:], second[:, HEAD_DIM:]], axis=1)

    out = pl.BlockSpec((step, cols, width), lambda i: (i, 0, 0))
    shape = jax.ShapeDtypeStruct((rows, cols, width), packed.dtype)
    return pl.pallas_call(
        body,
        grid=(2,),
        in_specs=[pl.BlockSpec((heads, step, cols, lanes), lambda i: (0, i, 0, 0))],
        out_specs=[out, out],
        out_shape=[shape, shape],
        compiler_params=params(SMALL_BYTES),
    )(packed)


def block_group(group, r, base, reach_class, w_first, w_last, kvw, kvt, qcw, dkv, sd, bias, qow):
    lanes = kvw.shape[-1]
    both = 2 * HALF
    scale = float(HEAD_DIM) ** -0.5
    lane = lax.broadcasted_iota(jnp.int32, (both, lanes), 1)
    off = REACH - reach_class
    width = HALF + 2 * reach_class
    taps = range(w_first, w_last)
    held = []
    for j in range(INTERLEAVE):
        block = group * INTERLEAVE + j
        start = pl.multiple_of(block * HALF, HALF)
        span = pl.ds(pl.multiple_of(start + off, 16), width)
        turned = pl.ds(pl.multiple_of(start - (j % 2) * HALF, both), WINDOW)
        rows_qc = jnp.concatenate(
            [qcw[r, pl.ds(start, HALF), :], qcw[r + 1, pl.ds(start, HALF), :]], axis=0)
        zero = jnp.zeros_like(rows_qc)
        qb = jnp.concatenate(
            [jnp.where(lane < HEAD_DIM, rows_qc * scale, zero),
             jnp.where(lane < HEAD_DIM, zero, rows_qc)], axis=0)
        held.append((start, span, turned, qb))
    tops = []
    for j in range(INTERLEAVE):
        _, span, _, qb = held[j]
        top = jnp.full((8, both), FAR, jnp.float32)
        for w in taps:
            product = lax.dot_general(kvw[base + w, span, :], qb, NT, preferred_element_type=jnp.float32)
            score = product[:, :both] + bias[w, off:off + width]
            sd[j, w, :width, :both] = score
            sd[j, w, :width, both:] = product[:, both:]
            top = jnp.maximum(top, jnp.max(score.reshape(width // 8, 8, both), axis=0))
        tops.append(jnp.max(top, axis=0, keepdims=True))
    sums = []
    for j in range(INTERLEAVE):
        total = jnp.zeros((8, both), jnp.float32)
        dot = jnp.zeros((8, both), jnp.float32)
        for w in taps:
            p = jnp.exp(sd[j, w, :width, :both] - tops[j])
            sd[j, w, :width, :both] = p
            total += jnp.sum(p.reshape(width // 8, 8, both), axis=0)
            dot += jnp.sum((p * sd[j, w, :width, both:]).reshape(width // 8, 8, both), axis=0)
        inverse = 1.0 / jnp.sum(total, axis=0, keepdims=True)
        sums.append((inverse, jnp.sum(dot, axis=0, keepdims=True) * inverse))
    edge = jnp.zeros((off, 2 * both), jnp.bfloat16)
    for j in range(INTERLEAVE):
        start, span, turned, qb = held[j]
        inverse, delta = sums[j]
        acc = jnp.zeros((lanes, 2 * both), jnp.float32)
        for w in taps:
            prob = sd[j, w, :width, :both] * inverse
            ds = (prob * (sd[j, w, :width, both:] - delta)).astype(jnp.bfloat16)
            dp = jnp.concatenate([ds, prob.astype(jnp.bfloat16)], axis=1)
            dkv[base + w, span, :] += jnp.dot(dp, qb, preferred_element_type=jnp.float32)
            if off:
                dp = jnp.concatenate([edge, dp, edge], axis=0)
            acc += jnp.dot(kvt[j % 2, base + w, :, turned], dp, preferred_element_type=jnp.float32)
        qo = jnp.concatenate([acc[:HEAD_DIM, :both] * scale, acc[HEAD_DIM:, both:]], axis=0)
        qo = qo.T.astype(jnp.bfloat16)
        qow[r, pl.ds(start, HALF), :] = qo[:HALF]
        qow[r + 1, pl.ds(start, HALF), :] = qo[HALF:]


def row_pairs(reach_ref, logw_ref, kvw, kvt, qcw, dkv, sd, bias, qow):
    blocks = qcw.shape[1] // HALF
    both = 2 * HALF

    @pl.loop(0, 4)
    def _(pair):
        r = 2 * pair
        base = r + jnp.where(pair >= 2, 2 * HALO, 0)
        key = lax.broadcasted_iota(jnp.int32, (WINDOW, both), 0) - REACH
        query = lax.broadcasted_iota(jnp.int32, (WINDOW, both), 1)
        second = query >= HALF
        gap = jnp.abs(key - jnp.where(second, query - HALF, query))
        near = gap <= jnp.where(second, reach_ref[r + 1], reach_ref[r])
        for w in range(TAPS):
            ok = near
            if w == 0:
                ok = near & jnp.logical_not(second)
            if w == TAPS - 1:
                ok = near & second
            bias[w] = jnp.where(ok, logw_ref[base + w], FAR)

        widest = jnp.maximum(reach_ref[r], reach_ref[r + 1])

        def run(when, reach_class, w_first, w_last):
            @pl.when(when)
            def _():
                @pl.loop(0, blocks // INTERLEAVE)
                def _(group):
                    block_group(group, r, base, reach_class, w_first, w_last,
                                kvw, kvt, qcw, dkv, sd, bias, qow)

        no_above = logw_ref[base + HALO - 1] < 0.5 * FAR
        no_below = logw_ref[base + TAPS - HALO] < 0.5 * FAR
        run(no_above, REACH, HALO, TAPS)
        run(no_below, REACH, 0, TAPS - HALO)
        rest = jnp.logical_not(no_above | no_below)
        below = 0
        for reach_class in CLASSES:
            run(rest & (widest > below) & (widest <= reach_class), reach_class, 0, TAPS)
            below = reach_class


def attend(second_half, reach, log_weight, kv, kv_partner, kv_plane, qc):
    _, sectors, rows, cols, lanes = kv.shape
    ring = sectors * cols
    padded = ring + 2 * REACH
    run = rows + 2 * HALO

    def body(half_ref, reach_ref, logw_ref, kv_ref, partner_ref, plane_ref, qc_ref,
             qo_ref, own_ref, to_partner_ref, to_plane_ref, kvw, kvt, qcw, dkv, sd, bias, qow):
        first = half_ref[0] == 0
        for s in range(sectors):
            at = slice(REACH + s * cols, REACH + (s + 1) * cols)
            for n in range(2):
                kvw[n * run + HALO:n * run + HALO + rows, at] = kv_ref[n, s]
                qcw[n * rows:(n + 1) * rows, s * cols:(s + 1) * cols] = qc_ref[n, s]

        @pl.when(first)
        def _():
            for s in range(sectors):
                at = slice(REACH + s * cols, REACH + (s + 1) * cols)
                kvw[0:2, at] = plane_ref[s]
                kvw[6:8, at] = partner_ref[0, s, 0:2]
                kvw[8:10, at] = partner_ref[0, s, 2:4]
                kvw[14:16, at] = partner_ref[1, s, 0:2]

        @pl.when(jnp.logical_not(first))
        def _():
            for s in range(sectors):
                at = slice(REACH + s * cols, REACH + (s + 1) * cols)
                kvw[0:2, at] = partner_ref[0, s, 2:4]
                kvw[6:8, at] = partner_ref[1, s, 0:2]
                kvw[8:10, at] = partner_ref[1, s, 2:4]
                kvw[14:16, at] = plane_ref[s]

        kvw[:, 0:REACH] = kvw[:, ring:ring + REACH]
        kvw[:, REACH + ring:padded] = kvw[:, REACH:2 * REACH]

        @pl.loop(0, 2 * run)
        def _(kr):
            kvt[0, kr] = kvw[kr].T
            kvt[1, kr, :, 0:padded - HALF] = kvw[kr, HALF:].T
            dkv[kr] = jnp.zeros((padded, lanes), jnp.float32)

        row_pairs(reach_ref, logw_ref, kvw, kvt, qcw, dkv, sd, bias, qow)

        dkv[:, ring:ring + REACH] += dkv[:, 0:REACH]
        dkv[:, REACH:2 * REACH] += dkv[:, REACH + ring:padded]
        for s in range(sectors):
            at = slice(REACH + s * cols, REACH + (s + 1) * cols)
            for n in range(2):
                qo_ref[n, s] = qow[n * rows:(n + 1) * rows, s * cols:(s + 1) * cols]
                own_ref[n, s] = dkv[n * run + HALO:n * run + HALO + rows, at].astype(jnp.bfloat16)

        @pl.when(first)
        def _():
            for s in range(sectors):
                at = slice(REACH + s * cols, REACH + (s + 1) * cols)
                to_partner_ref[s, 0:4] = dkv[6:10, at].astype(jnp.bfloat16)
                to_partner_ref[s, 4:6] = dkv[14:16, at].astype(jnp.bfloat16)
                to_plane_ref[s] = dkv[0:2, at].astype(jnp.bfloat16)

        @pl.when(jnp.logical_not(first))
        def _():
            for s in range(sectors):
                at = slice(REACH + s * cols, REACH + (s + 1) * cols)
                to_partner_ref[s, 0:2] = dkv[0:2, at].astype(jnp.bfloat16)
                to_partner_ref[s, 2:6] = dkv[6:10, at].astype(jnp.bfloat16)
                to_plane_ref[s] = dkv[14:16, at].astype(jnp.bfloat16)

    whole = jax.ShapeDtypeStruct(kv.shape, jnp.bfloat16)

    def out(count):
        return jax.ShapeDtypeStruct((sectors, count, cols, lanes), jnp.bfloat16)

    return pl.pallas_call(
        body,
        in_specs=[smem(), smem(), smem(), vmem(), vmem(), vmem(), vmem()],
        out_specs=[vmem()] * 4,
        out_shape=[whole, whole, out(3 * HALO), out(HALO)],
        scratch_shapes=[
            pltpu.VMEM((2 * run, padded, lanes), jnp.bfloat16),
            pltpu.VMEM((2, 2 * run, lanes, padded), jnp.bfloat16),
            pltpu.VMEM((2 * rows, ring, lanes), jnp.bfloat16),
            pltpu.VMEM((2 * run, padded, lanes), jnp.float32),
            pltpu.VMEM((INTERLEAVE, TAPS, WINDOW, 4 * HALF), jnp.float32),
            pltpu.VMEM((TAPS, WINDOW, 2 * HALF), jnp.float32),
            pltpu.VMEM((2 * rows, ring, lanes), jnp.bfloat16),
        ],
        compiler_params=params(VMEM_BYTES),
        cost_estimate=pl.CostEstimate(flops=40_000_000_000, bytes_accessed=10_000_000, transcendentals=5_000_000),
    )(second_half, reach, log_weight, kv, kv_partner, kv_plane, qc)


def add_home(second_half, own, partner, plane):
    runs, sectors, rows, cols, lanes = own.shape
    step = sectors // 4

    def body(half_ref, own_ref, partner_ref, plane_ref, out_ref):
        def add(order):
            for n, (ref, row) in enumerate(order):
                at = slice((n % 2) * HALO, (n % 2 + 1) * HALO)
                other = ref[:, row:row + HALO].astype(jnp.float32)
                out_ref[n // 2, :, at] = (own_ref[n // 2, :, at].astype(jnp.float32) + other).astype(out_ref.dtype)

        @pl.when(half_ref[0] == 0)
        def _():
            add([(plane_ref, 0), (partner_ref, 0), (partner_ref, 2), (partner_ref, 4)])

        @pl.when(half_ref[0] != 0)
        def _():
            add([(partner_ref, 0), (partner_ref, 2), (partner_ref, 4), (plane_ref, 0)])

    block = pl.BlockSpec((runs, step, rows, cols, lanes), lambda i: (0, i, 0, 0, 0))

    def side(count):
        return pl.BlockSpec((step, count, cols, lanes), lambda i: (i, 0, 0, 0))

    return pl.pallas_call(
        body,
        grid=(4,),
        in_specs=[smem(), block, side(3 * HALO), side(HALO)],
        out_specs=block,
        out_shape=jax.ShapeDtypeStruct(own.shape, own.dtype),
        compiler_params=params(SMALL_BYTES),
    )(second_half, own, partner, plane)


def exchange(packed):
    return lax.all_to_all(packed, ("band", "lon"), 0, 0)


def to_partner(block):
    return lax.ppermute(block, "lon", [(i, i ^ 1) for i in range(lax.axis_size("lon"))])


def to_next_plane(block):
    planes, columns = lax.axis_size("plane"), lax.axis_size("lon")
    route = []
    for plane in range(planes - 1):
        for i in range(1, columns, 2):
            here, there = plane * columns + i, (plane + 1) * columns + i - 1
            route += [(here, there), (there, here)]
    return lax.ppermute(block, ("plane", "lon"), route)


def on_device(queries, key_vectors, value_vectors, cotangent, quad_weight, lon_reach):
    rows, cols, _ = queries.shape
    half_rows = rows // 2
    bands, sectors = lax.axis_size("band"), lax.axis_size("lon")
    half = lax.axis_index("lon") % 2
    parted = (bands * sectors, half_rows, cols, 2 * HEAD_DIM)
    by_band = (bands, sectors, half_rows, cols, 2 * HEAD_DIM)

    other_reach = lax.ppermute(lon_reach, "band", [(0, 1), (1, 0)])
    lower = lax.axis_index("band") == 0
    reach = jnp.stack([jnp.where(lower, lon_reach, other_reach), jnp.where(lower, other_reach, lon_reach)])
    reach = lax.dynamic_slice_in_dim(reach, half * half_rows, half_rows, axis=1).reshape(-1)
    ext = (lax.axis_index("plane") * bands + jnp.arange(bands)[:, None]) * rows + half * half_rows - HALO
    ext = (ext + jnp.arange(half_rows + 2 * HALO)[None, :]).reshape(-1)
    inside = (ext >= 0) & (ext < quad_weight.shape[0])
    log_weight = jnp.where(inside, jnp.log(quad_weight[jnp.clip(ext, 0, quad_weight.shape[0] - 1)]), FAR)
    second_half = half.astype(jnp.int32).reshape(1)

    kv = exchange(pack_pair(key_vectors, value_vectors).reshape(parted)).reshape(by_band)
    rim = jnp.where(half == 0, kv[0, :, :HALO], kv[1, :, half_rows - HALO:])
    kv_plane = to_next_plane(rim)
    kv_partner = to_partner(kv)
    qc = exchange(pack_pair(queries, cotangent).reshape(parted)).reshape(by_band)
    qo, own, partner, plane = attend(second_half, reach, log_weight, kv, kv_partner, kv_plane, qc)
    plane = to_next_plane(plane)
    partner = to_partner(partner)
    packed = (HEADS, rows, cols, 2 * HEAD_DIM)
    grad_queries, attended = unpack_pair(exchange(qo.reshape(parted)).reshape(packed))
    total = add_home(second_half, own, partner, plane)
    grad_keys, grad_values = unpack_pair(exchange(total.reshape(parted)).reshape(packed))
    return attended, grad_queries, grad_keys, grad_values


def solution(mesh):
    bands, sectors = mesh.devices.shape
    planes = Mesh(mesh.devices.reshape(bands // 2, 2, sectors), ("plane", "band", "lon"))
    cells = P(("plane", "band"), "lon", None)
    return jax.shard_map(
        on_device,
        mesh=planes,
        in_specs=(cells, cells, cells, cells, P(), P(("plane", "band"))),
        out_specs=(cells, cells, cells, cells),
        check_vma=False,
    )
```
